128 devices in a mesh: space: 32 (over y, x, z_hi), shift: 4 (over z_lo, core).
Axes of the slice: x: 4, y: 4, z: 4 (z_hi: 2, z_lo: 2; z = z_hi * 2 + z_lo), core: 2. Of those that a mesh axis runs over, the one named last changes fastest.
Arguments:
- state: float32 [256, 256, 256], P('space'), may hold values from -13 to 13
- reaction: float32 [256, 256, 256], P('space'), may hold values from 0.05 to 0.5
Outputs:
- next_state: float32 [256, 256, 256], P(('space', 'shift'))
The draws below stay inside these ranges and needn't reach their ends.
All inputs are finite; a program needn't handle non-finite values.
Results may differ from the reference program's by a relative error of at most 0.00017.
Values sent between devices are 32-bit elements; how exact they have to be, the bound alone decides.
A program may use at most 192 MiB of HBM per device.

```python
import math
import jax
import jax.numpy as jnp
from jax import lax

NX = 256
NY = 256
ITERS = 3
NZ = 256
SHIFTS = 16


def draw_state(key, part):
    key = jax.random.fold_in(key, 11)
    planes = jnp.arange(NZ, dtype=jnp.float32)
    amplitude = 0.3 * jnp.exp(math.log(10.0) * planes / max(NZ - 1, 1))
    rough = jnp.clip(jax.random.normal(key, (NZ, NY, NX), jnp.float32), -4.0, 4.0)
    return amplitude[:, None, None] * rough


def steps_of(stream_key, dims, cuts, low, largest):
    gain, own = 1.0, jax.random.fold_in(stream_key, 6)
    for position, parts in cuts:
        draws = jnp.exp(jax.random.uniform(jax.random.fold_in(own, position), (parts,), jnp.float32, low / len(cuts), largest / len(cuts)))
        gain = gain * jnp.repeat(draws, dims[position] // parts).reshape([-1 if axis == position else 1 for axis in range(len(dims))])
    return gain


def setup_inputs(seed: int = 0) -> dict:
    streams_of = jax.random.split(jax.random.key(seed), 3)
    state = draw_state(jax.random.fold_in(streams_of[2], 71), 0)
    reaction = jnp.clip(jnp.exp(math.log(0.5) - 2.3025851 * jax.random.uniform(streams_of[1], (NZ, NY, NX), jnp.float32) ** steps_of(streams_of[1], (NZ, NY, NX), ((0, 32),), -0.2, 0.2)), 0.05, 0.5)
    return {"state": state, "reaction": reaction}


fraction = 0.4


def operate(field, diagonal):
    beside = jnp.roll(field, 1, 0) + jnp.roll(field, -1, 0)
    beside = beside + jnp.roll(field, 1, 1) + jnp.roll(field, -1, 1)
    beside = beside + jnp.roll(field, 1, 2) + jnp.roll(field, -1, 2)
    return diagonal * field - beside


def reference(state, reaction):
    spacing = 10.0 / SHIFTS
    coef = 2.0 * spacing * math.sin(math.pi * fraction) / math.pi

    def one_shift(total, node_index):
        node = spacing * (node_index.astype(jnp.float32) - SHIFTS / 2 + 0.5)
        diagonal = jnp.exp(node) + 6.0 + reaction
        solution = jnp.zeros_like(state)
        residual = state
        direction = state
        norm_now = jnp.sum(state * state)
        for step in range(ITERS):
            image = operate(direction, diagonal)
            alpha = norm_now / jnp.sum(direction * image)
            solution = solution + alpha * direction
            residual = residual - alpha * image
            norm_next = jnp.sum(residual * residual)
            direction = residual + (norm_next / norm_now) * direction
            norm_now = norm_next
        weight = coef * jnp.exp((1.0 - fraction) * node)
        return total + weight * solution, None

    total, unused = lax.scan(one_shift, jnp.zeros_like(state), jnp.arange(SHIFTS, dtype=jnp.int32))
    return total
```

```python
import functools
import math

import jax
import jax.numpy as jnp
from jax import lax
from jax.experimental import pallas as pl
from jax.experimental.pallas import tpu as pltpu
from jax.sharding import PartitionSpec as P

MESH = pl.DeviceIdType.MESH
SH_DEV = 4
FRACTION = 0.4
LOW, HIGH = 0.05, 12.5
PIECES = 4
PAD = 8


def two_sum(a, b):
    s = a + b
    t = s - a
    return s, (a - (s - t)) + (b - t)


def quick(s, e):
    t = s + e
    return t, e - (t - s)


def split(a):
    c = a * 4097.0
    h = c - (c - a)
    return h, a - h


def mul(a, b):
    p = a[0] * b[0]
    ah, al = split(a[0])
    bh, bl = split(b[0])
    e = ((ah * bh - p) + ah * bl + al * bh) + al * bl
    return quick(p, e + (a[0] * b[1] + a[1] * b[0]))


def add(a, b):
    s, e = two_sum(a[0], b[0])
    return quick(s, e + (a[1] + b[1]))


def neg(a):
    return -a[0], -a[1]


def sub(a, b):
    return add(a, neg(b))


def div(a, b):
    q = a[0] / b[0]
    r = sub(a, mul((q, jnp.zeros_like(q)), b))
    return quick(q, r[0] / b[0])


def clamp(a):
    inside = (a[0] >= LOW) & (a[0] <= HIGH)
    edge = jnp.where(a[0] < LOW, LOW, HIGH)
    return jnp.where(inside, a[0], edge), jnp.where(inside, a[1], 0.0)


def nonneg(a):
    keep = a[0] > 0.0
    return jnp.where(keep, a[0], 0.0), jnp.where(keep, a[1], 0.0)


def coefficients(m, shifts_all):
    one = jnp.ones_like(m[0][0])
    a0 = clamp(div(m[1], m[0]))
    g1 = nonneg(sub(m[2], mul(a0, m[1])))
    h1 = add(sub(m[3], mul((2.0 * a0[0], 2.0 * a0[1]), m[2])), mul(mul(a0, a0), m[1]))
    some1 = g1[0] > 0.0
    g1s = jnp.where(some1, g1[0], one), jnp.where(some1, g1[1], 0.0)
    a1 = clamp(div(h1, g1s))
    b1 = nonneg(div(g1, m[0]))
    s = neg(add(a0, a1))
    t = sub(mul(a0, a1), b1)
    r3 = add(m[4], add(mul(s, m[3]), mul(t, m[2])))
    g2 = nonneg(r3)
    h2 = add(add(m[5], mul(s, m[4])), add(mul(t, m[3]), mul(s, r3)))
    some2 = g2[0] > 0.0
    g2s = jnp.where(some2, g2[0], one)
    a0, a1, b1, t, s = a0[0], a1[0], b1[0], t[0], s[0]
    a2 = jnp.clip(h2[0] / g2s, LOW, HIGH)
    b1 = jnp.minimum(b1, jnp.maximum((HIGH - a0) * (a0 - LOW), 0.0))
    b2 = jnp.minimum(g2[0] / g1s[0], jnp.maximum((HIGH - a1) * (a1 - LOW), 0.0))

    lane = lax.broadcasted_iota(jnp.int32, one.shape, 1)
    spacing = 10.0 / shifts_all
    coef = 2.0 * spacing * math.sin(math.pi * FRACTION) / math.pi
    node = spacing * (jnp.minimum(lane, shifts_all - 1).astype(jnp.float32) - shifts_all / 2 + 0.5)
    weight = jnp.where(lane < shifts_all, coef * jnp.exp((1.0 - FRACTION) * node), 0.0)
    sigma = jnp.exp(node)
    d2 = sigma + a2
    d1 = jnp.maximum((sigma + a1) - b2 / d2, sigma + LOW)
    d0 = jnp.maximum((sigma + a0) - b1 / d1, sigma + LOW)
    y0 = weight / d0
    y1 = -y0 / d1
    y2 = -y1 / d2
    y0, y1, y2 = (jnp.sum(y, axis=1, keepdims=True) for y in (y0, y1, y2))
    a0, s, t = a0[:, :1], s[:, :1], t[:, :1]
    return y0 - a0 * y1 + t * y2, y1 + s * y2, y2


def kernel(
    n_space, n_shift, column, state, reaction, out,
    bb, rr, v1, v2, w0, recv_b, recv_v, recv_w, acc, tile, tiles, pair, pairs,
    load_b, load_r, send_x, got_b, got_v, got_w, send_1, got_1, send_2, got_2,
):
    space, member = lax.axis_index("space"), lax.axis_index("shift")
    planes, rows, width = state.shape
    piece = rows // PIECES
    half = n_shift // 2
    high = member // half
    is_outer = (member % (n_shift - 1)) == 0
    outer = jnp.where(is_outer, 1, 0)
    depth = 2 * (1 - outer)

    def plane(k):
        return k + high * (planes - 1 - 2 * k)

    step = 2 * high - 1
    partner = (lax.rem(space + step + n_space, n_space), (n_shift - 1) * (1 - high))
    deep = column // n_shift
    here = lax.rem(space, deep) * n_shift + member
    column_at = space // deep
    columns = n_space // deep

    def beside(k):
        other = lax.rem(here + k, column)
        return column_at * deep + other // n_shift, lax.rem(other, n_shift)

    def across(k):
        return lax.rem(column_at + k, columns) * deep + lax.rem(space, deep), member

    barrier = pltpu.get_barrier_semaphore()

    @pl.when(is_outer)
    def _():
        pl.semaphore_signal(barrier, inc=1, device_id=partner, device_id_type=MESH)

    for k in range(1, column):
        pl.semaphore_signal(barrier, inc=1, device_id=beside(k), device_id_type=MESH)
    for k in range(1, columns):
        pl.semaphore_signal(barrier, inc=1, device_id=across(k), device_id_type=MESH)

    def get_b(j):
        return pltpu.make_async_copy(
            state.at[plane(depth - 2 + j)], bb.at[j, pl.ds(PAD, rows)], load_b.at[j])

    def get_r(j):
        return pltpu.make_async_copy(reaction.at[plane(depth - 1 + j)], rr.at[j], load_r.at[j])

    @pl.when(is_outer)
    def _():
        for j in range(2, 7):
            get_b(j).start()
        for j in range(1, 5):
            get_r(j).start()

    @pl.when(jnp.logical_not(is_outer))
    def _():
        for j in range(7):
            get_b(j).start()
        for j in range(5):
            get_r(j).start()

    acc[...] = jnp.zeros_like(acc)
    tile[...] = jnp.zeros_like(tile)
    pl.semaphore_wait(barrier, column + columns - 2 + outer)

    def wrap(ref, j):
        ref[j, PAD - 1 : PAD] = ref[j, PAD + rows - 1 : PAD + rows]
        ref[j, PAD + rows : PAD + rows + 1] = ref[j, PAD : PAD + 1]

    def at(ref, j, c, shift=0):
        return ref[j, pl.ds(PAD + c * piece + shift, piece)]

    def rows_of(c, start=0):
        first = c * piece + start
        return pl.ds(first if isinstance(c, int) else pl.multiple_of(first, 8), piece)

    def put(ref, j, c, value):
        ref[j, rows_of(c, PAD)] = value

    def coef_at(j, c):
        return rr[j, rows_of(c)] + 6.0

    def flat(ref, j, c):
        return ref[j, rows_of(c, PAD)]

    def applied(ref, j, c, r, sides):
        x = flat(ref, j, c)
        near = at(ref, j, c, -1) + at(ref, j, c, 1)
        near = near + pltpu.roll(x, 1, 1) + pltpu.roll(x, width - 1, 1)
        for side in sides:
            near = near + flat(ref, side, c)
        return coef_at(r, c) * x - near

    def gather(k, product):
        acc[k] += jnp.sum(product.reshape(piece // 8, 8, width), axis=0)

    def each(body):
        for c in range(PIECES):
            body(c)

    def make_v1(j, sides):
        each(lambda c: put(v1, j, c, applied(bb, j + 1, c, j, sides)))
        wrap(v1, j)

    def make_v2(k, sides):
        each(lambda c: put(v2, k, c, applied(v1, k + 1, c, k + 1, sides)))

    def early(j):
        def body(c):
            b, v = flat(bb, j, c), flat(v1, j - 1, c)
            gather(0, b * b)
            gather(1, b * v)
            gather(2, v * v)

        each(body)

    def late(k):
        def body(c):
            v, u = flat(v1, k + 1, c), flat(v2, k, c)
            gather(3, v * u)
            gather(4, u * u)

        each(body)

    def last(k, scale):
        def body(c):
            u = flat(v2, k, c)
            near = pltpu.roll(u, width - 1, 1) + at(v2, k, c, 1)
            near = near + scale * flat(v2, k + 1, c)
            gather(5, u * (coef_at(k + 1, c) * u - 2.0 * near))

        each(body)

    @pl.when(jnp.logical_not(is_outer))
    def _():
        for j in range(7):
            get_b(j).wait()
        for j in range(1, 6):
            wrap(bb, j)
        for j in range(5):
            get_r(j).wait()
        for j in range(5):
            make_v1(j, (j, j + 2))
        for k in range(3):
            make_v2(k, (k, k + 2))
        for k in range(2):
            wrap(v2, k)
            early(k + 2)
            late(k)
        last(0, 1.0)
        last(1, 0.5)

    @pl.when(is_outer)
    def _():
        def send_b(c):
            return pltpu.make_async_remote_copy(
                src_ref=state.at[plane(0), pl.ds(c * piece, piece)], dst_ref=recv_b.at[c],
                send_sem=send_x.at[c], recv_sem=got_b.at[c],
                device_id=partner, device_id_type=MESH)

        def send_v(c):
            return pltpu.make_async_remote_copy(
                src_ref=v1.at[1, pl.ds(PAD + c * piece, piece)], dst_ref=recv_v.at[c],
                send_sem=send_x.at[PIECES + c], recv_sem=got_v.at[c],
                device_id=partner, device_id_type=MESH)

        def send_w(i):
            return pltpu.make_async_remote_copy(
                src_ref=w0.at[2 * i + high], dst_ref=recv_w.at[i],
                send_sem=send_x.at[2 * PIECES + i], recv_sem=got_w.at[i],
                device_id=partner, device_id_type=MESH)

        for c in range(PIECES):
            send_b(c).start()
        for j in range(2, 7):
            get_b(j).wait()
        for j in range(2, 6):
            wrap(bb, j)
        for j in range(1, 5):
            get_r(j).wait()
        make_v1(1, (3,))
        for j in range(2, 5):
            make_v1(j, (j, j + 2))
        make_v2(2, (2, 4))
        make_v2(1, (3,))
        early(3)
        for c in range(PIECES):
            send_b(c).wait_recv()
            b = flat(bb, 2, c)
            v = flat(v1, 1, c) - recv_b[c]
            put(v1, 1, c, v)
            send_v(c).start()
            gather(0, b * b)
            gather(1, b * v)
            gather(2, v * v)
        wrap(v1, 1)

        def own_w(c):
            w0[c] = applied(v1, 1, c, 1, (2,))

        for i in range(PIECES // 2):
            own_w(2 * i)
            own_w(2 * i + 1)
            send_w(i).start()
        each(lambda c: put(v2, 1, c, flat(v2, 1, c) - flat(v1, 1, c)))
        wrap(v2, 1)
        late(1)
        last(1, 1.0)
        for c in range(PIECES):
            send_v(c).wait_recv()
            u = w0[c] - recv_v[c]
            put(v2, 0, c, u)
            gather(3, flat(v1, 1, c) * u)
            gather(4, u * u)
        wrap(v2, 0)
        last(0, 1.0)
        for i in range(PIECES // 2):
            c = 2 * i + 1 - high
            send_w(i).wait_recv()
            gather(5, -2.0 * flat(v2, 0, c) * (recv_w[i] - flat(v1, 1, c)))
        for c in range(PIECES):
            send_b(c).wait_send()
            send_v(c).wait_send()
        for i in range(PIECES // 2):
            send_w(i).wait_send()

    for k in range(6):
        row = acc[k]
        row = row[:, : width // 2] + row[:, width // 2 :]
        tile[k : k + 1] = jnp.sum(row, axis=0, keepdims=True)

    def step_1(k):
        return pltpu.make_async_remote_copy(
            src_ref=tile, dst_ref=tiles.at[k], send_sem=send_1.at[k], recv_sem=got_1.at[k],
            device_id=beside(k), device_id_type=MESH)

    def step_2(k):
        return pltpu.make_async_remote_copy(
            src_ref=pair, dst_ref=pairs.at[k], send_sem=send_2.at[k], recv_sem=got_2.at[k],
            device_id=across(k), device_id_type=MESH)

    for k in range(1, column):
        step_1(k).start()
    hi, lo = tile[...], jnp.zeros(tile.shape, jnp.float32)
    for k in range(1, column):
        step_1(k).wait_recv()
        hi, e = two_sum(hi, tiles[k])
        lo = lo + e
    pair[0] = hi
    pair[1] = lo
    for k in range(1, columns):
        step_2(k).start()
    for k in range(1, columns):
        step_2(k).wait_recv()
        hi, e = two_sum(hi, pairs[k, 0])
        lo = lo + (e + pairs[k, 1])
    turn = hi.shape[1] // 2
    while turn:
        hi, e = two_sum(hi, pltpu.roll(hi, turn, 1))
        lo = (lo + pltpu.roll(lo, turn, 1)) + e
        turn //= 2
    hi, lo = quick(hi, lo)
    moments = [(hi[k : k + 1], lo[k : k + 1]) for k in range(6)]
    c0, c1, c2 = coefficients(moments, SH_DEV * n_shift)

    for k in range(2):
        def body(c, k=k):
            value = c0 * flat(bb, k + 2, c) + c1 * flat(v1, k + 1, c) + c2 * flat(v2, k, c)
            out[k + high * (1 - 2 * k), rows_of(c)] = value

        each(body)
    for k in range(1, column):
        step_1(k).wait_send()
    for k in range(1, columns):
        step_2(k).wait_send()


def on_device(state, reaction):
    n_space, n_shift = lax.axis_size("space"), lax.axis_size("shift")
    planes, rows, width = state.shape
    column = 2 * n_shift
    columns = n_space * n_shift // column
    piece = rows // PIECES
    f32 = jnp.float32
    padded = rows + 2 * PAD
    dma = pltpu.SemaphoreType.DMA
    cells = 2 * rows * width
    return pl.pallas_call(
        functools.partial(kernel, n_space, n_shift, column),
        out_shape=jax.ShapeDtypeStruct((planes // n_shift, rows, width), f32),
        in_specs=[pl.BlockSpec(memory_space=pl.ANY)] * 2,
        out_specs=pl.BlockSpec(memory_space=pltpu.VMEM),
        scratch_shapes=[
            pltpu.VMEM((7, padded, width), f32),
            pltpu.VMEM((5, rows, width), f32),
            pltpu.VMEM((5, padded, width), f32),
            pltpu.VMEM((3, padded, width), f32),
            pltpu.VMEM((PIECES, piece, width), f32),
            pltpu.VMEM((PIECES, piece, width), f32),
            pltpu.VMEM((PIECES, piece, width), f32),
            pltpu.VMEM((PIECES // 2, piece, width), f32),
            pltpu.VMEM((6, 8, width), f32),
            pltpu.VMEM((8, width // 2), f32),
            pltpu.VMEM((column, 8, width // 2), f32),
            pltpu.VMEM((2, 8, width // 2), f32),
            pltpu.VMEM((columns, 2, 8, width // 2), f32),
            dma((7,)),
            dma((5,)),
            dma((2 * PIECES + PIECES // 2,)),
            dma((PIECES,)),
            dma((PIECES,)),
            dma((PIECES // 2,)),
            dma((column,)),
            dma((column,)),
            dma((columns,)),
            dma((columns,)),
        ],
        compiler_params=pltpu.CompilerParams(
            collective_id=0, has_side_effects=True, vmem_limit_bytes=60 * 2**20),
        cost_estimate=pl.CostEstimate(
            flops=100 * cells, bytes_accessed=40 * cells, transcendentals=0),
    )(state, reaction)


def solution(mesh):
    in_specs = (P("space", None, None), P("space", None, None))
    out_specs = P(("space", "shift"), None, None)
    return jax.shard_map(
        on_device, mesh=mesh, in_specs=in_specs, out_specs=out_specs, check_vma=False
    )
```

```python
import functools
import math

import jax
import jax.numpy as jnp
from jax import lax
from jax.experimental import pallas as pl
from jax.experimental.pallas import tpu as pltpu
from jax.sharding import PartitionSpec as P

MESH = pl.DeviceIdType.MESH
SH_DEV = 4
FRACTION = 0.4
LOW, HIGH = 0.05, 12.5
PIECES = 4
PAD = 8


def two_sum(a, b):
    s = a + b
    t = s - a
    return s, (a - (s - t)) + (b - t)


def quick(s, e):
    t = s + e
    return t, e - (t - s)


def split(a):
    c = a * 4097.0
    h = c - (c - a)
    return h, a - h


def mul(a, b):
    p = a[0] * b[0]
    ah, al = split(a[0])
    bh, bl = split(b[0])
    e = ((ah * bh - p) + ah * bl + al * bh) + al * bl
    return quick(p, e + (a[0] * b[1] + a[1] * b[0]))


def add(a, b):
    s, e = two_sum(a[0], b[0])
    return quick(s, e + (a[1] + b[1]))


def neg(a):
    return -a[0], -a[1]


def sub(a, b):
    return add(a, neg(b))


def div(a, b):
    q = a[0] / b[0]
    r = sub(a, mul((q, jnp.zeros_like(q)), b))
    return quick(q, r[0] / b[0])


def clamp(a):
    inside = (a[0] >= LOW) & (a[0] <= HIGH)
    edge = jnp.where(a[0] < LOW, LOW, HIGH)
    return jnp.where(inside, a[0], edge), jnp.where(inside, a[1], 0.0)


def nonneg(a):
    keep = a[0] > 0.0
    return jnp.where(keep, a[0], 0.0), jnp.where(keep, a[1], 0.0)


def coefficients(m, shifts_all):
    one = jnp.ones_like(m[0][0])
    a0 = clamp(div(m[1], m[0]))
    g1 = nonneg(sub(m[2], mul(a0, m[1])))
    h1 = add(sub(m[3], mul((2.0 * a0[0], 2.0 * a0[1]), m[2])), mul(mul(a0, a0), m[1]))
    some1 = g1[0] > 0.0
    g1s = jnp.where(some1, g1[0], one), jnp.where(some1, g1[1], 0.0)
    a1 = clamp(div(h1, g1s))
    b1 = nonneg(div(g1, m[0]))
    s = neg(add(a0, a1))
    t = sub(mul(a0, a1), b1)
    r3 = add(m[4], add(mul(s, m[3]), mul(t, m[2])))
    g2 = nonneg(r3)
    h2 = add(add(m[5], mul(s, m[4])), add(mul(t, m[3]), mul(s, r3)))
    some2 = g2[0] > 0.0
    g2s = jnp.where(some2, g2[0], one)
    a0, a1, b1, t, s = a0[0], a1[0], b1[0], t[0], s[0]
    a2 = jnp.clip(h2[0] / g2s, LOW, HIGH)
    b1 = jnp.minimum(b1, jnp.maximum((HIGH - a0) * (a0 - LOW), 0.0))
    b2 = jnp.minimum(g2[0] / g1s[0], jnp.maximum((HIGH - a1) * (a1 - LOW), 0.0))

    lane = lax.broadcasted_iota(jnp.int32, one.shape, 1)
    spacing = 10.0 / shifts_all
    coef = 2.0 * spacing * math.sin(math.pi * FRACTION) / math.pi
    node = spacing * (jnp.minimum(lane, shifts_all - 1).astype(jnp.float32) - shifts_all / 2 + 0.5)
    weight = jnp.where(lane < shifts_all, coef * jnp.exp((1.0 - FRACTION) * node), 0.0)
    sigma = jnp.exp(node)
    d2 = sigma + a2
    d1 = jnp.maximum((sigma + a1) - b2 / d2, sigma + LOW)
    d0 = jnp.maximum((sigma + a0) - b1 / d1, sigma + LOW)
    y0 = weight / d0
    y1 = -y0 / d1
    y2 = -y1 / d2
    y0, y1, y2 = (jnp.sum(y, axis=1, keepdims=True) for y in (y0, y1, y2))
    a0, s, t = a0[:, :1], s[:, :1], t[:, :1]
    return y0 - a0 * y1 + t * y2, y1 + s * y2, y2


def kernel(
    n_space, n_shift, column, state, reaction, out,
    bb, rr, v1, v2, w0, recv_b, recv_v, recv_w, acc, tile, tiles, pair, pairs,
    load_b, load_r, send_x, got_b, got_v, got_w, send_1, got_1, send_2, got_2,
):
    space, member = lax.axis_index("space"), lax.axis_index("shift")
    planes, rows, width = state.shape
    piece = rows // PIECES
    half = n_shift // 2
    high = member // half
    is_outer = (member % (n_shift - 1)) == 0
    outer = jnp.where(is_outer, 1, 0)
    depth = 2 * (1 - outer)

    def plane(k):
        return k + high * (planes - 1 - 2 * k)

    step = 2 * high - 1
    partner = (lax.rem(space + step + n_space, n_space), (n_shift - 1) * (1 - high))
    deep = column // n_shift
    here = lax.rem(space, deep) * n_shift + member
    column_at = space // deep
    columns = n_space // deep

    def beside(k):
        other = lax.rem(here + k, column)
        return column_at * deep + other // n_shift, lax.rem(other, n_shift)

    def across(k):
        return lax.rem(column_at + k, columns) * deep + lax.rem(space, deep), member

    barrier = pltpu.get_barrier_semaphore()

    @pl.when(is_outer)
    def _():
        pl.semaphore_signal(barrier, inc=1, device_id=partner, device_id_type=MESH)

    for k in range(1, column):
        pl.semaphore_signal(barrier, inc=1, device_id=beside(k), device_id_type=MESH)
    for k in range(1, columns):
        pl.semaphore_signal(barrier, inc=1, device_id=across(k), device_id_type=MESH)

    def get_b(j):
        return pltpu.make_async_copy(
            state.at[plane(depth - 2 + j)], bb.at[j, pl.ds(PAD, rows)], load_b.at[j])

    def get_r(j):
        return pltpu.make_async_copy(reaction.at[plane(depth - 1 + j)], rr.at[j], load_r.at[j])

    @pl.when(is_outer)
    def _():
        for j in range(2, 7):
            get_b(j).start()
        for j in range(1, 5):
            get_r(j).start()

    @pl.when(jnp.logical_not(is_outer))
    def _():
        for j in range(7):
            get_b(j).start()
        for j in range(5):
            get_r(j).start()

    acc[...] = jnp.zeros_like(acc)
    tile[...] = jnp.zeros_like(tile)
    pl.semaphore_wait(barrier, column + columns - 2 + outer)

    def wrap(ref, j):
        ref[j, PAD - 1 : PAD] = ref[j, PAD + rows - 1 : PAD + rows]
        ref[j, PAD + rows : PAD + rows + 1] = ref[j, PAD : PAD + 1]

    def at(ref, j, c, shift=0):
        return ref[j, pl.ds(PAD + c * piece + shift, piece)]

    def rows_of(c, start=0):
        first = c * piece + start
        return pl.ds(first if isinstance(c, int) else pl.multiple_of(first, 8), piece)

    def put(ref, j, c, value):
        ref[j, rows_of(c, PAD)] = value

    def coef_at(j, c):
        return rr[j, rows_of(c)] + 6.0

    def flat(ref, j, c):
        return ref[j, rows_of(c, PAD)]

    def applied(ref, j, c, r, sides):
        x = flat(ref, j, c)
        near = at(ref, j, c, -1) + at(ref, j, c, 1)
        near = near + pltpu.roll(x, 1, 1) + pltpu.roll(x, width - 1, 1)
        for side in sides:
            near = near + flat(ref, side, c)
        return coef_at(r, c) * x - near

    def gather(k, product):
        acc[k] += jnp.sum(product.reshape(piece // 8, 8, width), axis=0)

    def each(body):
        for c in range(PIECES):
            body(c)

    def make_v1(j, sides):
        each(lambda c: put(v1, j, c, applied(bb, j + 1, c, j, sides)))
        wrap(v1, j)

    def make_v2(k, sides):
        each(lambda c: put(v2, k, c, applied(v1, k + 1, c, k + 1, sides)))

    def early(j):
        def body(c):
            b, v = flat(bb, j, c), flat(v1, j - 1, c)
            gather(0, b * b)
            gather(1, b * v)
            gather(2, v * v)

        each(body)

    def late(k):
        def body(c):
            v, u = flat(v1, k + 1, c), flat(v2, k, c)
            gather(3, v * u)
            gather(4, u * u)

        each(body)

    def last(k, scale):
        def body(c):
            u = flat(v2, k, c)
            near = pltpu.roll(u, width - 1, 1) + at(v2, k, c, 1)
            near = near + scale * flat(v2, k + 1, c)
            gather(5, u * (coef_at(k + 1, c) * u - 2.0 * near))

        each(body)

    @pl.when(jnp.logical_not(is_outer))
    def _():
        for j in range(7):
            get_b(j).wait()
        for j in range(1, 6):
            wrap(bb, j)
        for j in range(5):
            get_r(j).wait()
        for j in range(5):
            make_v1(j, (j, j + 2))
        for k in range(3):
            make_v2(k, (k, k + 2))
        for k in range(2):
            wrap(v2, k)
            early(k + 2)
            late(k)
        last(0, 1.0)
        last(1, 0.5)

    @pl.when(is_outer)
    def _():
        def send_b(c):
            return pltpu.make_async_remote_copy(
                src_ref=state.at[plane(0), pl.ds(c * piece, piece)], dst_ref=recv_b.at[c],
                send_sem=send_x.at[c], recv_sem=got_b.at[c],
                device_id=partner, device_id_type=MESH)

        def send_v(c):
            return pltpu.make_async_remote_copy(
                src_ref=v1.at[1, pl.ds(PAD + c * piece, piece)], dst_ref=recv_v.at[c],
                send_sem=send_x.at[PIECES + c], recv_sem=got_v.at[c],
                device_id=partner, device_id_type=MESH)

        def send_w(i):
            return pltpu.make_async_remote_copy(
                src_ref=w0.at[2 * i + high], dst_ref=recv_w.at[i],
                send_sem=send_x.at[2 * PIECES + i], recv_sem=got_w.at[i],
                device_id=partner, device_id_type=MESH)

        for c in range(PIECES):
            send_b(c).start()
        for j in range(2, 7):
            get_b(j).wait()
        for j in range(2, 6):
            wrap(bb, j)
        for j in range(1, 5):
            get_r(j).wait()
        make_v1(1, (3,))
        for j in range(2, 5):
            make_v1(j, (j, j + 2))
        make_v2(2, (2, 4))
        make_v2(1, (3,))
        early(3)
        for c in range(PIECES):
            send_b(c).wait_recv()
            b = flat(bb, 2, c)
            v = flat(v1, 1, c) - recv_b[c]
            put(v1, 1, c, v)
            send_v(c).start()
            gather(0, b * b)
            gather(1, b * v)
            gather(2, v * v)
        wrap(v1, 1)

        def own_w(c):
            w0[c] = applied(v1, 1, c, 1, (2,))

        for i in range(PIECES // 2):
            own_w(2 * i)
            own_w(2 * i + 1)
            send_w(i).start()
        each(lambda c: put(v2, 1, c, flat(v2, 1, c) - flat(v1, 1, c)))
        wrap(v2, 1)
        late(1)
        last(1, 1.0)
        for c in range(PIECES):
            send_v(c).wait_recv()
            u = w0[c] - recv_v[c]
            put(v2, 0, c, u)
            gather(3, flat(v1, 1, c) * u)
            gather(4, u * u)
        wrap(v2, 0)
        last(0, 1.0)
        for i in range(PIECES // 2):
            c = 2 * i + 1 - high
            send_w(i).wait_recv()
            gather(5, -2.0 * flat(v2, 0, c) * (recv_w[i] - flat(v1, 1, c)))
        for c in range(PIECES):
            send_b(c).wait_send()
            send_v(c).wait_send()
        for i in range(PIECES // 2):
            send_w(i).wait_send()

    for k in range(6):
        row = acc[k]
        row = row[:, : width // 2] + row[:, width // 2 :]
        tile[k : k + 1] = jnp.sum(row, axis=0, keepdims=True)

    def step_1(k):
        return pltpu.make_async_remote_copy(
            src_ref=tile, dst_ref=tiles.at[k], send_sem=send_1.at[k], recv_sem=got_1.at[k],
            device_id=beside(k), device_id_type=MESH)

    def step_2(k):
        return pltpu.make_async_remote_copy(
            src_ref=pair, dst_ref=pairs.at[k], send_sem=send_2.at[k], recv_sem=got_2.at[k],
            device_id=across(k), device_id_type=MESH)

    for k in range(1, column):
        step_1(k).start()
    hi, lo = tile[...], jnp.zeros(tile.shape, jnp.float32)
    for k in range(1, column):
        step_1(k).wait_recv()
        hi, e = two_sum(hi, tiles[k])
        lo = lo + e
    pair[0] = hi
    pair[1] = lo
    for k in range(1, columns):
        step_2(k).start()
    for k in range(1, columns):
        step_2(k).wait_recv()
        hi, e = two_sum(hi, pairs[k, 0])
        lo = lo + (e + pairs[k, 1])
    turn = hi.shape[1] // 2
    while turn:
        hi, e = two_sum(hi, pltpu.roll(hi, turn, 1))
        lo = (lo + pltpu.roll(lo, turn, 1)) + e
        turn //= 2
    hi, lo = quick(hi, lo)
    moments = [(hi[k : k + 1], lo[k : k + 1]) for k in range(6)]
    c0, c1, c2 = coefficients(moments, SH_DEV * n_shift)

    for k in range(2):
        def body(c, k=k):
            value = c0 * flat(bb, k + 2, c) + c1 * flat(v1, k + 1, c) + c2 * flat(v2, k, c)
            out[k + high * (1 - 2 * k), rows_of(c)] = value

        each(body)
    for k in range(1, column):
        step_1(k).wait_send()
    for k in range(1, columns):
        step_2(k).wait_send()


def on_device(state, reaction):
    n_space, n_shift = lax.axis_size("space"), lax.axis_size("shift")
    planes, rows, width = state.shape
    column = 2 * n_shift
    columns = n_space * n_shift // column
    piece = rows // PIECES
    f32 = jnp.float32
    padded = rows + 2 * PAD
    dma = pltpu.SemaphoreType.DMA
    cells = 2 * rows * width
    return pl.pallas_call(
        functools.partial(kernel, n_space, n_shift, column),
        out_shape=pltpu.VMEM((planes // n_shift, rows, width), f32),
        in_specs=[pl.BlockSpec(memory_space=pltpu.HBM)] * 2,
        out_specs=pl.BlockSpec(memory_space=pltpu.VMEM),
        scratch_shapes=[
            pltpu.VMEM((7, padded, width), f32),
            pltpu.VMEM((5, rows, width), f32),
            pltpu.VMEM((5, padded, width), f32),
            pltpu.VMEM((3, padded, width), f32),
            pltpu.VMEM((PIECES, piece, width), f32),
            pltpu.VMEM((PIECES, piece, width), f32),
            pltpu.VMEM((PIECES, piece, width), f32),
            pltpu.VMEM((PIECES // 2, piece, width), f32),
            pltpu.VMEM((6, 8, width), f32),
            pltpu.VMEM((8, width // 2), f32),
            pltpu.VMEM((column, 8, width // 2), f32),
            pltpu.VMEM((2, 8, width // 2), f32),
            pltpu.VMEM((columns, 2, 8, width // 2), f32),
            dma((7,)),
            dma((5,)),
            dma((2 * PIECES + PIECES // 2,)),
            dma((PIECES,)),
            dma((PIECES,)),
            dma((PIECES // 2,)),
            dma((column,)),
            dma((column,)),
            dma((columns,)),
            dma((columns,)),
        ],
        compiler_params=pltpu.CompilerParams(
            collective_id=0, has_side_effects=True, vmem_limit_bytes=58 * 2**20),
        cost_estimate=pl.CostEstimate(
            flops=100 * cells, bytes_accessed=40 * cells, transcendentals=0),
    )(state, reaction)


def solution(mesh):
    in_specs = (P("space", None, None), P("space", None, None))
    out_specs = P(("space", "shift"), None, None)
    return jax.shard_map(
        on_device, mesh=mesh, in_specs=in_specs, out_specs=out_specs, check_vma=False
    )
```

```python
import functools
import math

import jax
import jax.numpy as jnp
from jax import lax
from jax.experimental import pallas as pl
from jax.experimental.pallas import tpu as pltpu
from jax.sharding import PartitionSpec as P

MESH = pl.DeviceIdType.MESH
SH_DEV = 4
FRACTION = 0.4
LOW, HIGH = 0.05, 12.5
PIECES = 4
PAD = 8


def two_sum(a, b):
    s = a + b
    t = s - a
    return s, (a - (s - t)) + (b - t)


def quick(s, e):
    t = s + e
    return t, e - (t - s)


def split(a):
    c = a * 4097.0
    h = c - (c - a)
    return h, a - h


def mul(a, b):
    p = a[0] * b[0]
    ah, al = split(a[0])
    bh, bl = split(b[0])
    e = ((ah * bh - p) + ah * bl + al * bh) + al * bl
    return quick(p, e + (a[0] * b[1] + a[1] * b[0]))


def add(a, b):
    s, e = two_sum(a[0], b[0])
    return quick(s, e + (a[1] + b[1]))


def neg(a):
    return -a[0], -a[1]


def sub(a, b):
    return add(a, neg(b))


def div(a, b):
    q = a[0] / b[0]
    r = sub(a, mul((q, jnp.zeros_like(q)), b))
    return quick(q, r[0] / b[0])


def clamp(a):
    inside = (a[0] >= LOW) & (a[0] <= HIGH)
    edge = jnp.where(a[0] < LOW, LOW, HIGH)
    return jnp.where(inside, a[0], edge), jnp.where(inside, a[1], 0.0)


def nonneg(a):
    keep = a[0] > 0.0
    return jnp.where(keep, a[0], 0.0), jnp.where(keep, a[1], 0.0)


def coefficients(m, shifts_all):
    one = jnp.ones_like(m[0][0])
    a0 = clamp(div(m[1], m[0]))
    g1 = nonneg(sub(m[2], mul(a0, m[1])))
    h1 = add(sub(m[3], mul((2.0 * a0[0], 2.0 * a0[1]), m[2])), mul(mul(a0, a0), m[1]))
    some1 = g1[0] > 0.0
    g1s = jnp.where(some1, g1[0], one), jnp.where(some1, g1[1], 0.0)
    a1 = clamp(div(h1, g1s))
    b1 = nonneg(div(g1, m[0]))
    s = neg(add(a0, a1))
    t = sub(mul(a0, a1), b1)
    r3 = add(m[4], add(mul(s, m[3]), mul(t, m[2])))
    g2 = nonneg(r3)
    h2 = add(add(m[5], mul(s, m[4])), add(mul(t, m[3]), mul(s, r3)))
    some2 = g2[0] > 0.0
    g2s = jnp.where(some2, g2[0], one)
    a0, a1, b1, t, s = a0[0], a1[0], b1[0], t[0], s[0]
    a2 = jnp.clip(h2[0] / g2s, LOW, HIGH)
    b1 = jnp.minimum(b1, jnp.maximum((HIGH - a0) * (a0 - LOW), 0.0))
    b2 = jnp.minimum(g2[0] / g1s[0], jnp.maximum((HIGH - a1) * (a1 - LOW), 0.0))

    lane = lax.broadcasted_iota(jnp.int32, one.shape, 1)
    spacing = 10.0 / shifts_all
    coef = 2.0 * spacing * math.sin(math.pi * FRACTION) / math.pi
    node = spacing * (jnp.minimum(lane, shifts_all - 1).astype(jnp.float32) - shifts_all / 2 + 0.5)
    weight = jnp.where(lane < shifts_all, coef * jnp.exp((1.0 - FRACTION) * node), 0.0)
    sigma = jnp.exp(node)
    d2 = sigma + a2
    d1 = jnp.maximum((sigma + a1) - b2 / d2, sigma + LOW)
    d0 = jnp.maximum((sigma + a0) - b1 / d1, sigma + LOW)
    y0 = weight / d0
    y1 = -y0 / d1
    y2 = -y1 / d2
    y0, y1, y2 = (jnp.sum(y, axis=1, keepdims=True) for y in (y0, y1, y2))
    a0, s, t = a0[:, :1], s[:, :1], t[:, :1]
    return y0 - a0 * y1 + t * y2, y1 + s * y2, y2


def kernel(
    n_space, n_shift, column, state, reaction, out,
    bb, rr, v1, v2, u0, w0, p0, recv_b, recv_u, recv_p, recv_r, acc, tile, tiles, pair, pairs,
    load_b, load_r, send_x, got_b, got_u, got_p, got_r, send_1, got_1, send_2, got_2,
):
    space, member = lax.axis_index("space"), lax.axis_index("shift")
    planes, rows, width = state.shape
    piece = rows // PIECES
    half = n_shift // 2
    high = member // half
    is_outer = (member % (n_shift - 1)) == 0
    outer = jnp.where(is_outer, 1, 0)
    depth = 2 * (1 - outer)

    def plane(k):
        return k + high * (planes - 1 - 2 * k)

    step = 2 * high - 1
    partner = (lax.rem(space + step + n_space, n_space), (n_shift - 1) * (1 - high))
    deep = column // n_shift
    here = lax.rem(space, deep) * n_shift + member
    column_at = space // deep
    columns = n_space // deep

    def beside(k):
        other = lax.rem(here + k, column)
        return column_at * deep + other // n_shift, lax.rem(other, n_shift)

    def across(k):
        return lax.rem(column_at + k, columns) * deep + lax.rem(space, deep), member

    barrier = pltpu.get_barrier_semaphore()

    @pl.when(is_outer)
    def _():
        pl.semaphore_signal(barrier, inc=1, device_id=partner, device_id_type=MESH)

    for k in range(1, column):
        pl.semaphore_signal(barrier, inc=1, device_id=beside(k), device_id_type=MESH)
    for k in range(1, columns):
        pl.semaphore_signal(barrier, inc=1, device_id=across(k), device_id_type=MESH)

    def get_b(j):
        return pltpu.make_async_copy(
            state.at[plane(depth - 2 + j)], bb.at[j, pl.ds(PAD, rows)], load_b.at[j])

    def get_r(j):
        return pltpu.make_async_copy(reaction.at[plane(depth - 1 + j)], rr.at[j], load_r.at[j])

    @pl.when(is_outer)
    def _():
        for j in range(2, 7):
            get_b(j).start()
        for j in range(1, 5):
            get_r(j).start()

    @pl.when(jnp.logical_not(is_outer))
    def _():
        for j in range(7):
            get_b(j).start()
        for j in range(5):
            get_r(j).start()

    acc[...] = jnp.zeros_like(acc)
    pl.semaphore_wait(barrier, column + columns - 2 + outer)

    def wrap(ref, j):
        ref[j, PAD - 1 : PAD] = ref[j, PAD + rows - 1 : PAD + rows]
        ref[j, PAD + rows : PAD + rows + 1] = ref[j, PAD : PAD + 1]

    def at(ref, j, c, shift=0):
        return ref[j, pl.ds(PAD + c * piece + shift, piece)]

    def rows_of(c, start=0):
        first = c * piece + start
        return pl.ds(first if isinstance(c, int) else pl.multiple_of(first, 8), piece)

    def put(ref, j, c, value):
        ref[j, rows_of(c, PAD)] = value

    def coef_at(j, c):
        return rr[j, rows_of(c)] + 6.0

    def flat(ref, j, c):
        return ref[j, rows_of(c, PAD)]

    def applied(ref, j, c, r, sides):
        x = flat(ref, j, c)
        near = at(ref, j, c, -1) + at(ref, j, c, 1)
        near = near + pltpu.roll(x, 1, 1) + pltpu.roll(x, width - 1, 1)
        for side in sides:
            near = near + flat(ref, side, c)
        return coef_at(r, c) * x - near

    def gather(k, product):
        acc[k] += jnp.sum(product.reshape(piece // 8, 8, width), axis=0)

    def each(body):
        for c in range(PIECES):
            body(c)

    def make_v1(j, sides):
        each(lambda c: put(v1, j, c, applied(bb, j + 1, c, j, sides)))
        wrap(v1, j)

    def make_v2(k, sides):
        each(lambda c: put(v2, k, c, applied(v1, k + 1, c, k + 1, sides)))

    def early(j):
        def body(c):
            b, v = flat(bb, j, c), flat(v1, j - 1, c)
            gather(0, b * b)
            gather(1, b * v)
            gather(2, v * v)

        each(body)

    def late(k):
        def body(c):
            v, u = flat(v1, k + 1, c), flat(v2, k, c)
            gather(3, v * u)
            gather(4, u * u)

        each(body)

    def last(k, scale):
        def body(c):
            u = flat(v2, k, c)
            near = pltpu.roll(u, width - 1, 1) + at(v2, k, c, 1)
            near = near + scale * flat(v2, k + 1, c)
            gather(5, u * (coef_at(k + 1, c) * u - 2.0 * near))

        each(body)

    @pl.when(jnp.logical_not(is_outer))
    def _():
        for j in range(7):
            get_b(j).wait()
        for j in range(1, 6):
            wrap(bb, j)
        for j in range(5):
            get_r(j).wait()
        for j in range(5):
            make_v1(j, (j, j + 2))
        for k in range(3):
            make_v2(k, (k, k + 2))
        for k in range(2):
            wrap(v2, k)
            early(k + 2)
            late(k)
        last(0, 1.0)
        last(1, 0.5)

    @pl.when(is_outer)
    def _():
        def send_b(c):
            return pltpu.make_async_remote_copy(
                src_ref=state.at[plane(0), pl.ds(c * piece, piece)], dst_ref=recv_b.at[c],
                send_sem=send_x.at[c], recv_sem=got_b.at[c],
                device_id=partner, device_id_type=MESH)

        def send_u(c):
            return pltpu.make_async_remote_copy(
                src_ref=u0.at[0, pl.ds(PAD + c * piece, piece)], dst_ref=recv_u.at[c],
                send_sem=send_x.at[PIECES + c], recv_sem=got_u.at[c],
                device_id=partner, device_id_type=MESH)

        def send_p(c):
            return pltpu.make_async_remote_copy(
                src_ref=p0.at[c], dst_ref=recv_p.at[c],
                send_sem=send_x.at[2 * PIECES + c], recv_sem=got_p.at[c],
                device_id=partner, device_id_type=MESH)

        def send_r(c):
            return pltpu.make_async_remote_copy(
                src_ref=reaction.at[plane(0), pl.ds(c * piece, piece)], dst_ref=recv_r.at[c],
                send_sem=send_x.at[3 * PIECES + c], recv_sem=got_r.at[c],
                device_id=partner, device_id_type=MESH)

        late_half = lax.rem(space, 2) == 1
        early_half = jnp.logical_not(late_half)
        from_late, from_early = range(PIECES - 1), range(PIECES - 1, PIECES)

        for c in range(PIECES):
            send_b(c).start()
        for j in range(2, 7):
            get_b(j).wait()
        wrap(bb, 2)
        for j in range(1, 5):
            get_r(j).wait()
        for c in range(PIECES):
            put(u0, 0, c, applied(bb, 2, c, 1, (3,)))
            send_u(c).start()
        wrap(u0, 0)
        for j in range(3, 6):
            wrap(bb, j)
        make_v1(2, (2, 4))

        def own_p(c):
            p0[c] = applied(u0, 0, c, 1, ()) - flat(v1, 2, c)

        @pl.when(late_half)
        def _():
            for c in from_late:
                own_p(c)
                send_p(c).start()
                send_r(c).start()

        @pl.when(early_half)
        def _():
            for c in from_early:
                own_p(c)
                send_p(c).start()
                send_r(c).start()

        for j in range(3, 5):
            make_v1(j, (j, j + 2))
        make_v2(2, (2, 4))
        make_v2(1, (3,))
        early(3)
        for c in range(PIECES):
            send_b(c).wait_recv()
            b = flat(bb, 2, c)
            v = flat(u0, 0, c) - recv_b[c]
            put(v1, 1, c, v)
            gather(0, b * b)
            gather(1, b * v)
            gather(2, v * v)
        wrap(v1, 1)
        for c in range(PIECES):
            w0[c] = applied(v1, 1, c, 1, (2,))
        each(lambda c: put(v2, 1, c, flat(v2, 1, c) - flat(v1, 1, c)))
        wrap(v2, 1)
        late(1)
        last(1, 1.0)
        for c in range(PIECES):
            send_u(c).wait_recv()
            u = w0[c] - (recv_u[c] - flat(bb, 2, c))
            put(v2, 0, c, u)
            gather(3, flat(v1, 1, c) * u)
            gather(4, u * u)
        wrap(v2, 0)
        last(0, 1.0)

        def edge(c):
            send_p(c).wait_recv()
            send_r(c).wait_recv()
            b = flat(bb, 2, c)
            near = at(bb, 2, c, -1) + at(bb, 2, c, 1)
            near = near + pltpu.roll(b, 1, 1) + pltpu.roll(b, width - 1, 1)
            far = recv_p[c] - ((recv_r[c] + 6.0) * b - near) - flat(v1, 1, c)
            gather(5, -2.0 * flat(v2, 0, c) * far)

        @pl.when(early_half)
        def _():
            for c in from_late:
                edge(c)

        @pl.when(late_half)
        def _():
            for c in from_early:
                edge(c)

        for c in range(PIECES):
            send_b(c).wait_send()
            send_u(c).wait_send()

        @pl.when(late_half)
        def _():
            for c in from_late:
                send_p(c).wait_send()
                send_r(c).wait_send()

        @pl.when(early_half)
        def _():
            for c in from_early:
                send_p(c).wait_send()
                send_r(c).wait_send()

    lanes = width // 2
    hi = jnp.zeros((8, lanes), jnp.float32)
    lane = lax.broadcasted_iota(jnp.int32, hi.shape, 1)
    line = lax.broadcasted_iota(jnp.int32, hi.shape, 0)
    for k in range(6):
        row = acc[k]
        row = jnp.sum(row[:, :lanes] + row[:, lanes:], axis=0, keepdims=True)
        hi = jnp.where(line == k, row, hi)
    lo = jnp.zeros_like(hi)
    turn = lanes // 2
    while turn:
        hi, e = two_sum(hi, pltpu.roll(hi, turn, 1))
        lo = (lo + pltpu.roll(lo, turn, 1)) + e
        turn //= 2
    packed = jnp.where(lane == line, hi, 0.0) + jnp.where(lane == line + 8, lo, 0.0)
    tile[...] = jnp.sum(packed, axis=0, keepdims=True)

    def merge(total, lost):
        return total + jnp.where(lane[:1] >= 8, pltpu.roll(lost, 8, 1), 0.0)

    def step_1(k):
        return pltpu.make_async_remote_copy(
            src_ref=tile, dst_ref=tiles.at[k], send_sem=send_1.at[k], recv_sem=got_1.at[k],
            device_id=beside(k), device_id_type=MESH)

    def step_2(k):
        return pltpu.make_async_remote_copy(
            src_ref=pair, dst_ref=pairs.at[k], send_sem=send_2.at[k], recv_sem=got_2.at[k],
            device_id=across(k), device_id_type=MESH)

    for k in range(1, column):
        step_1(k).start()
    total, lost = tile[...], jnp.zeros(tile.shape, jnp.float32)
    for k in range(1, column):
        step_1(k).wait_recv()
        total, e = two_sum(total, tiles[k])
        lost = lost + e
    pair[...] = merge(total, lost)
    for k in range(1, columns):
        step_2(k).start()
    total, lost = pair[...], jnp.zeros(tile.shape, jnp.float32)
    for k in range(1, columns):
        step_2(k).wait_recv()
        total, e = two_sum(total, pairs[k])
        lost = lost + e
    total = jnp.broadcast_to(merge(total, lost), hi.shape)
    hi = jnp.sum(jnp.where(lane == line, total, 0.0), axis=1, keepdims=True)
    lo = jnp.sum(jnp.where(lane == line + 8, total, 0.0), axis=1, keepdims=True)
    hi, lo = jnp.broadcast_to(hi, lane.shape), jnp.broadcast_to(lo, lane.shape)
    hi, lo = quick(hi, lo)
    moments = [(hi[k : k + 1], lo[k : k + 1]) for k in range(6)]
    c0, c1, c2 = coefficients(moments, SH_DEV * n_shift)

    for k in range(2):
        def body(c, k=k):
            value = c0 * flat(bb, k + 2, c) + c1 * flat(v1, k + 1, c) + c2 * flat(v2, k, c)
            out[k + high * (1 - 2 * k), rows_of(c)] = value

        each(body)
    for k in range(1, column):
        step_1(k).wait_send()
    for k in range(1, columns):
        step_2(k).wait_send()


def on_device(state, reaction):
    n_space, n_shift = lax.axis_size("space"), lax.axis_size("shift")
    planes, rows, width = state.shape
    column = 2 * n_shift
    columns = n_space * n_shift // column
    piece = rows // PIECES
    f32 = jnp.float32
    padded = rows + 2 * PAD
    dma = pltpu.SemaphoreType.DMA
    cells = 2 * rows * width
    return pl.pallas_call(
        functools.partial(kernel, n_space, n_shift, column),
        out_shape=pltpu.VMEM((planes // n_shift, rows, width), f32),
        in_specs=[pl.BlockSpec(memory_space=pltpu.HBM)] * 2,
        out_specs=pl.BlockSpec(memory_space=pltpu.VMEM),
        scratch_shapes=[
            pltpu.VMEM((7, padded, width), f32),
            pltpu.VMEM((5, rows, width), f32),
            pltpu.VMEM((5, padded, width), f32),
            pltpu.VMEM((3, padded, width), f32),
            pltpu.VMEM((1, padded, width), f32),
            pltpu.VMEM((PIECES, piece, width), f32),
            pltpu.VMEM((PIECES, piece, width), f32),
            pltpu.VMEM((PIECES, piece, width), f32),
            pltpu.VMEM((PIECES, piece, width), f32),
            pltpu.VMEM((PIECES, piece, width), f32),
            pltpu.VMEM((PIECES, piece, width), f32),
            pltpu.VMEM((6, 8, width), f32),
            pltpu.VMEM((1, width // 2), f32),
            pltpu.VMEM((column, 1, width // 2), f32),
            pltpu.VMEM((1, width // 2), f32),
            pltpu.VMEM((columns, 1, width // 2), f32),
            dma((7,)),
            dma((5,)),
            dma((4 * PIECES,)),
            dma((PIECES,)),
            dma((PIECES,)),
            dma((PIECES,)),
            dma((PIECES,)),
            dma((column,)),
            dma((column,)),
            dma((columns,)),
            dma((columns,)),
        ],
        compiler_params=pltpu.CompilerParams(
            collective_id=0, has_side_effects=True, vmem_limit_bytes=58 * 2**20),
        cost_estimate=pl.CostEstimate(
            flops=100 * cells, bytes_accessed=40 * cells, transcendentals=0),
    )(state, reaction)


def solution(mesh):
    in_specs = (P("space", None, None), P("space", None, None))
    out_specs = P(("space", "shift"), None, None)
    return jax.shard_map(
        on_device, mesh=mesh, in_specs=in_specs, out_specs=out_specs, check_vma=False
    )
```

```python
import functools
import math

import jax
import jax.numpy as jnp
from jax import lax
from jax.experimental import pallas as pl
from jax.experimental.pallas import tpu as pltpu
from jax.sharding import PartitionSpec as P

MESH = pl.DeviceIdType.MESH
SH_DEV = 4
FRACTION = 0.4
LOW, HIGH = 0.05, 12.5
PIECES = 4
PAD = 8


def two_sum(a, b):
    s = a + b
    t = s - a
    return s, (a - (s - t)) + (b - t)


def quick(s, e):
    t = s + e
    return t, e - (t - s)


def split(a):
    c = a * 4097.0
    h = c - (c - a)
    return h, a - h


def mul(a, b):
    p = a[0] * b[0]
    ah, al = split(a[0])
    bh, bl = split(b[0])
    e = ((ah * bh - p) + ah * bl + al * bh) + al * bl
    return quick(p, e + (a[0] * b[1] + a[1] * b[0]))


def add(a, b):
    s, e = two_sum(a[0], b[0])
    return quick(s, e + (a[1] + b[1]))


def neg(a):
    return -a[0], -a[1]


def sub(a, b):
    return add(a, neg(b))


def div(a, b):
    q = a[0] / b[0]
    r = sub(a, mul((q, jnp.zeros_like(q)), b))
    return quick(q, r[0] / b[0])


def clamp(a):
    inside = (a[0] >= LOW) & (a[0] <= HIGH)
    edge = jnp.where(a[0] < LOW, LOW, HIGH)
    return jnp.where(inside, a[0], edge), jnp.where(inside, a[1], 0.0)


def nonneg(a):
    keep = a[0] > 0.0
    return jnp.where(keep, a[0], 0.0), jnp.where(keep, a[1], 0.0)


def coefficients(m, shifts_all):
    one = jnp.ones_like(m[0][0])
    a0 = clamp(div(m[1], m[0]))
    g1 = nonneg(sub(m[2], mul(a0, m[1])))
    h1 = add(sub(m[3], mul((2.0 * a0[0], 2.0 * a0[1]), m[2])), mul(mul(a0, a0), m[1]))
    some1 = g1[0] > 0.0
    g1s = jnp.where(some1, g1[0], one), jnp.where(some1, g1[1], 0.0)
    a1 = clamp(div(h1, g1s))
    b1 = nonneg(div(g1, m[0]))
    s = neg(add(a0, a1))
    t = sub(mul(a0, a1), b1)
    r3 = add(m[4], add(mul(s, m[3]), mul(t, m[2])))
    g2 = nonneg(r3)
    h2 = add(add(m[5], mul(s, m[4])), add(mul(t, m[3]), mul(s, r3)))
    some2 = g2[0] > 0.0
    g2s = jnp.where(some2, g2[0], one)
    a0, a1, b1, t, s = a0[0], a1[0], b1[0], t[0], s[0]
    a2 = jnp.clip(h2[0] / g2s, LOW, HIGH)
    b1 = jnp.minimum(b1, jnp.maximum((HIGH - a0) * (a0 - LOW), 0.0))
    b2 = jnp.minimum(g2[0] / g1s[0], jnp.maximum((HIGH - a1) * (a1 - LOW), 0.0))

    lane = lax.broadcasted_iota(jnp.int32, one.shape, 1)
    spacing = 10.0 / shifts_all
    coef = 2.0 * spacing * math.sin(math.pi * FRACTION) / math.pi
    node = spacing * (jnp.minimum(lane, shifts_all - 1).astype(jnp.float32) - shifts_all / 2 + 0.5)
    weight = jnp.where(lane < shifts_all, coef * jnp.exp((1.0 - FRACTION) * node), 0.0)
    sigma = jnp.exp(node)
    d2 = sigma + a2
    d1 = jnp.maximum((sigma + a1) - b2 / d2, sigma + LOW)
    d0 = jnp.maximum((sigma + a0) - b1 / d1, sigma + LOW)
    y0 = weight / d0
    y1 = -y0 / d1
    y2 = -y1 / d2
    y0, y1, y2 = (jnp.sum(y, axis=1, keepdims=True) for y in (y0, y1, y2))
    a0, s, t = a0[:, :1], s[:, :1], t[:, :1]
    return y0 - a0 * y1 + t * y2, y1 + s * y2, y2


def kernel(
    n_space, n_shift, column, state, reaction, out,
    bb, rr, v1, v2, u0, w0, p0, recv_b, recv_u, recv_p, recv_r, acc, tile, tiles, pair, pairs,
    load_b, load_r, send_x, got_b, got_u, got_p, got_r, send_1, got_1, send_2, got_2,
):
    space, member = lax.axis_index("space"), lax.axis_index("shift")
    planes, rows, width = state.shape
    piece = rows // PIECES
    half = n_shift // 2
    high = member // half
    is_outer = (member % (n_shift - 1)) == 0
    outer = jnp.where(is_outer, 1, 0)
    depth = 2 * (1 - outer)

    def plane(k):
        return k + high * (planes - 1 - 2 * k)

    step = 2 * high - 1
    partner = (lax.rem(space + step + n_space, n_space), (n_shift - 1) * (1 - high))
    deep = column // n_shift
    chips = column // 2
    side = math.isqrt(n_space // deep)
    z, core = lax.rem(space, deep) * half + high, lax.rem(member, 2)
    y, x = space // deep // side, lax.rem(space // deep, side)

    def hops(distance, size):
        return min(distance, size - distance)

    up = sorted(
        ((dz, dc) for dz in range(chips) for dc in range(2) if dz + dc),
        key=lambda d: (-hops(d[0], chips), d))
    wide = sorted(
        ((dy, dx) for dy in range(side) for dx in range(side) if dy + dx),
        key=lambda d: (-hops(d[0], side) - hops(d[1], side), d))

    def beside(k):
        dz, dc = up[k]
        z2 = lax.rem(z + dz, chips)
        return space - lax.rem(space, deep) + z2 // half, lax.rem(z2, half) * 2 + lax.rem(core + dc, 2)

    def across(k):
        dy, dx = wide[k]
        chip = lax.rem(y + dy, side) * side + lax.rem(x + dx, side)
        return chip * deep + lax.rem(space, deep), member

    barrier = pltpu.get_barrier_semaphore()

    @pl.when(is_outer)
    def _():
        pl.semaphore_signal(barrier, inc=1, device_id=partner, device_id_type=MESH)

    for k in range(len(wide)):
        pl.semaphore_signal(barrier, inc=1, device_id=across(k), device_id_type=MESH)
    for k in range(len(up)):
        pl.semaphore_signal(barrier, inc=1, device_id=beside(k), device_id_type=MESH)
    pl.semaphore_wait(barrier, len(up) + len(wide) + outer)

    def get_b(j):
        return pltpu.make_async_copy(
            state.at[plane(depth - 2 + j)], bb.at[j, pl.ds(PAD, rows)], load_b.at[j])

    def get_r(j):
        return pltpu.make_async_copy(reaction.at[plane(depth - 1 + j)], rr.at[j], load_r.at[j])

    acc[...] = jnp.zeros_like(acc)

    def wrap(ref, j):
        ref[j, PAD - 1 : PAD] = ref[j, PAD + rows - 1 : PAD + rows]
        ref[j, PAD + rows : PAD + rows + 1] = ref[j, PAD : PAD + 1]

    def at(ref, j, c, shift=0):
        return ref[j, pl.ds(PAD + c * piece + shift, piece)]

    def rows_of(c, start=0):
        first = c * piece + start
        return pl.ds(first if isinstance(c, int) else pl.multiple_of(first, 8), piece)

    def put(ref, j, c, value):
        ref[j, rows_of(c, PAD)] = value

    def coef_at(j, c):
        return rr[j, rows_of(c)] + 6.0

    def flat(ref, j, c):
        return ref[j, rows_of(c, PAD)]

    def applied(ref, j, c, r, sides):
        x = flat(ref, j, c)
        near = at(ref, j, c, -1) + at(ref, j, c, 1)
        near = near + pltpu.roll(x, 1, 1) + pltpu.roll(x, width - 1, 1)
        for side in sides:
            near = near + flat(ref, side, c)
        return coef_at(r, c) * x - near

    def gather(k, product):
        acc[k] += jnp.sum(product.reshape(piece // 8, 8, width), axis=0)

    def each(body):
        for c in range(PIECES):
            body(c)

    def make_v1(j, sides):
        each(lambda c: put(v1, j, c, applied(bb, j + 1, c, j, sides)))
        wrap(v1, j)

    def make_v2(k, sides):
        each(lambda c: put(v2, k, c, applied(v1, k + 1, c, k + 1, sides)))

    def early(j):
        def body(c):
            b, v = flat(bb, j, c), flat(v1, j - 1, c)
            gather(0, b * b)
            gather(1, b * v)
            gather(2, v * v)

        each(body)

    def late(k):
        def body(c):
            v, u = flat(v1, k + 1, c), flat(v2, k, c)
            gather(3, v * u)
            gather(4, u * u)

        each(body)

    def last(k, scale):
        def body(c):
            u = flat(v2, k, c)
            near = pltpu.roll(u, width - 1, 1) + at(v2, k, c, 1)
            near = near + scale * flat(v2, k + 1, c)
            gather(5, u * (coef_at(k + 1, c) * u - 2.0 * near))

        each(body)

    @pl.when(jnp.logical_not(is_outer))
    def _():
        for j in range(7):
            get_b(j).start()
        for j in range(5):
            get_r(j).start()
        for j in range(7):
            get_b(j).wait()
        for j in range(1, 6):
            wrap(bb, j)
        for j in range(5):
            get_r(j).wait()
        for j in range(5):
            make_v1(j, (j, j + 2))
        for k in range(3):
            make_v2(k, (k, k + 2))
        for k in range(2):
            wrap(v2, k)
            early(k + 2)
            late(k)
        last(0, 1.0)
        last(1, 0.5)

    @pl.when(is_outer)
    def _():
        def send_b(c):
            return pltpu.make_async_remote_copy(
                src_ref=state.at[plane(0), pl.ds(c * piece, piece)], dst_ref=recv_b.at[c],
                send_sem=send_x.at[c], recv_sem=got_b.at[c],
                device_id=partner, device_id_type=MESH)

        def send_u(c):
            return pltpu.make_async_remote_copy(
                src_ref=u0.at[0, pl.ds(PAD + c * piece, piece)], dst_ref=recv_u.at[c],
                send_sem=send_x.at[PIECES + c], recv_sem=got_u.at[c],
                device_id=partner, device_id_type=MESH)

        def send_p(c):
            return pltpu.make_async_remote_copy(
                src_ref=p0.at[c], dst_ref=recv_p.at[c],
                send_sem=send_x.at[2 * PIECES + c], recv_sem=got_p.at[c],
                device_id=partner, device_id_type=MESH)

        def send_r(c):
            return pltpu.make_async_remote_copy(
                src_ref=reaction.at[plane(0), pl.ds(c * piece, piece)], dst_ref=recv_r.at[c],
                send_sem=send_x.at[3 * PIECES + c], recv_sem=got_r.at[c],
                device_id=partner, device_id_type=MESH)

        late_half = lax.rem(space, 2) == 1
        early_half = jnp.logical_not(late_half)
        from_late, from_early = range(PIECES - 1), range(PIECES - 1, PIECES)

        for c in range(PIECES):
            send_b(c).start()
        for j in range(2, 7):
            get_b(j).start()
        for j in range(1, 5):
            get_r(j).start()
        for j in range(2, 7):
            get_b(j).wait()
        wrap(bb, 2)
        for j in range(1, 5):
            get_r(j).wait()
        for c in range(PIECES):
            put(u0, 0, c, applied(bb, 2, c, 1, (3,)))
            send_u(c).start()
        wrap(u0, 0)
        for j in range(3, 6):
            wrap(bb, j)
        make_v1(2, (2, 4))

        def own_p(c):
            p0[c] = applied(u0, 0, c, 1, ()) - flat(v1, 2, c)

        @pl.when(late_half)
        def _():
            for c in from_late:
                own_p(c)
                send_p(c).start()
                send_r(c).start()

        @pl.when(early_half)
        def _():
            for c in from_early:
                own_p(c)
                send_p(c).start()
                send_r(c).start()

        for j in range(3, 5):
            make_v1(j, (j, j + 2))
        make_v2(2, (2, 4))
        make_v2(1, (3,))
        early(3)
        for c in range(PIECES):
            send_b(c).wait_recv()
            b = flat(bb, 2, c)
            v = flat(u0, 0, c) - recv_b[c]
            put(v1, 1, c, v)
            gather(0, b * b)
            gather(1, b * v)
            gather(2, v * v)
        wrap(v1, 1)
        for c in range(PIECES):
            w0[c] = applied(v1, 1, c, 1, (2,))
        each(lambda c: put(v2, 1, c, flat(v2, 1, c) - flat(v1, 1, c)))
        wrap(v2, 1)
        late(1)
        last(1, 1.0)
        for c in range(PIECES):
            send_u(c).wait_recv()
            u = w0[c] - (recv_u[c] - flat(bb, 2, c))
            put(v2, 0, c, u)
            gather(3, flat(v1, 1, c) * u)
            gather(4, u * u)
        wrap(v2, 0)
        last(0, 1.0)

        def edge(c):
            send_p(c).wait_recv()
            send_r(c).wait_recv()
            b = flat(bb, 2, c)
            near = at(bb, 2, c, -1) + at(bb, 2, c, 1)
            near = near + pltpu.roll(b, 1, 1) + pltpu.roll(b, width - 1, 1)
            far = recv_p[c] - ((recv_r[c] + 6.0) * b - near) - flat(v1, 1, c)
            gather(5, -2.0 * flat(v2, 0, c) * far)

        @pl.when(early_half)
        def _():
            for c in from_late:
                edge(c)

        @pl.when(late_half)
        def _():
            for c in from_early:
                edge(c)

        for c in range(PIECES):
            send_b(c).wait_send()
            send_u(c).wait_send()

        @pl.when(late_half)
        def _():
            for c in from_late:
                send_p(c).wait_send()
                send_r(c).wait_send()

        @pl.when(early_half)
        def _():
            for c in from_early:
                send_p(c).wait_send()
                send_r(c).wait_send()

    lanes = width // 2
    hi = jnp.zeros((8, lanes), jnp.float32)
    lane = lax.broadcasted_iota(jnp.int32, hi.shape, 1)
    line = lax.broadcasted_iota(jnp.int32, hi.shape, 0)
    for k in range(6):
        row = acc[k]
        row = jnp.sum(row[:, :lanes] + row[:, lanes:], axis=0, keepdims=True)
        hi = jnp.where(line == k, row, hi)
    lo = jnp.zeros_like(hi)
    turn = lanes // 2
    while turn:
        hi, e = two_sum(hi, pltpu.roll(hi, turn, 1))
        lo = (lo + pltpu.roll(lo, turn, 1)) + e
        turn //= 2
    packed = jnp.where(lane == line, hi, 0.0) + jnp.where(lane == line + 8, lo, 0.0)
    tile[...] = jnp.sum(packed, axis=0, keepdims=True)

    def merge(total, lost):
        return total + jnp.where(lane[:1] >= 8, pltpu.roll(lost, 8, 1), 0.0)

    def row_to(source, rows, k, send, got, to):
        return pltpu.make_async_remote_copy(
            src_ref=source, dst_ref=rows.at[k], send_sem=send, recv_sem=got,
            device_id=to, device_id_type=MESH)

    def all_rows(rows, send, got):
        return pltpu.make_async_remote_copy(
            src_ref=rows, dst_ref=rows, send_sem=send, recv_sem=got,
            device_id=across(0), device_id_type=MESH)

    def summed(own, rows):
        total, lost = own, jnp.zeros(own.shape, jnp.float32)
        for k in range(rows.shape[0]):
            total, e = two_sum(total, rows[k])
            lost = lost + e
        return merge(total, lost)

    for k in range(len(up)):
        row_to(tile, tiles, k, send_1, got_1, beside(k)).start()
    all_rows(tiles, send_1, got_1).wait_recv()
    pair[...] = summed(tile[...], tiles)
    for k in range(len(wide)):
        row_to(pair, pairs, k, send_2, got_2, across(k)).start()
    all_rows(pairs, send_2, got_2).wait_recv()
    total = summed(pair[...], pairs)
    total = jnp.broadcast_to(total, hi.shape)
    hi = jnp.sum(jnp.where(lane == line, total, 0.0), axis=1, keepdims=True)
    lo = jnp.sum(jnp.where(lane == line + 8, total, 0.0), axis=1, keepdims=True)
    hi, lo = jnp.broadcast_to(hi, lane.shape), jnp.broadcast_to(lo, lane.shape)
    hi, lo = quick(hi, lo)
    moments = [(hi[k : k + 1], lo[k : k + 1]) for k in range(6)]
    c0, c1, c2 = coefficients(moments, SH_DEV * n_shift)

    for k in range(2):
        def body(c, k=k):
            value = c0 * flat(bb, k + 2, c) + c1 * flat(v1, k + 1, c) + c2 * flat(v2, k, c)
            out[k + high * (1 - 2 * k), rows_of(c)] = value

        each(body)
    all_rows(tiles, send_1, got_1).wait_send()
    all_rows(pairs, send_2, got_2).wait_send()


def on_device(state, reaction):
    n_space, n_shift = lax.axis_size("space"), lax.axis_size("shift")
    planes, rows, width = state.shape
    column = 2 * n_shift
    columns = n_space * n_shift // column
    piece = rows // PIECES
    f32 = jnp.float32
    padded = rows + 2 * PAD
    dma = pltpu.SemaphoreType.DMA
    cells = 2 * rows * width
    return pl.pallas_call(
        functools.partial(kernel, n_space, n_shift, column),
        out_shape=pltpu.VMEM((planes // n_shift, rows, width), f32),
        in_specs=[pl.BlockSpec(memory_space=pltpu.HBM)] * 2,
        out_specs=pl.BlockSpec(memory_space=pltpu.VMEM),
        scratch_shapes=[
            pltpu.VMEM((7, padded, width), f32),
            pltpu.VMEM((5, rows, width), f32),
            pltpu.VMEM((5, padded, width), f32),
            pltpu.VMEM((3, padded, width), f32),
            pltpu.VMEM((1, padded, width), f32),
            pltpu.VMEM((PIECES, piece, width), f32),
            pltpu.VMEM((PIECES, piece, width), f32),
            pltpu.VMEM((PIECES, piece, width), f32),
            pltpu.VMEM((PIECES, piece, width), f32),
            pltpu.VMEM((PIECES, piece, width), f32),
            pltpu.VMEM((PIECES, piece, width), f32),
            pltpu.VMEM((6, 8, width), f32),
            pltpu.VMEM((1, width // 2), f32),
            pltpu.VMEM((column - 1, 1, width // 2), f32),
            pltpu.VMEM((1, width // 2), f32),
            pltpu.VMEM((columns - 1, 1, width // 2), f32),
            dma((7,)),
            dma((5,)),
            dma((4 * PIECES,)),
            dma((PIECES,)),
            dma((PIECES,)),
            dma((PIECES,)),
            dma((PIECES,)),
            dma,
            dma,
            dma,
            dma,
        ],
        compiler_params=pltpu.CompilerParams(
            collective_id=0, has_side_effects=True, vmem_limit_bytes=58 * 2**20),
        cost_estimate=pl.CostEstimate(
            flops=100 * cells, bytes_accessed=40 * cells, transcendentals=0),
    )(state, reaction)


def solution(mesh):
    in_specs = (P("space", None, None), P("space", None, None))
    out_specs = P(("space", "shift"), None, None)
    return jax.shard_map(
        on_device, mesh=mesh, in_specs=in_specs, out_specs=out_specs, check_vma=False
    )
```

```python
import functools
import math

import jax
import jax.numpy as jnp
from jax import lax
from jax.experimental import pallas as pl
from jax.experimental.pallas import tpu as pltpu
from jax.sharding import PartitionSpec as P

MESH = pl.DeviceIdType.MESH
SH_DEV = 4
FRACTION = 0.4
LOW, HIGH = 0.05, 12.5
PIECES = 4
PAD = 8


def two_sum(a, b):
    s = a + b
    t = s - a
    return s, (a - (s - t)) + (b - t)


def quick(s, e):
    t = s + e
    return t, e - (t - s)


def split(a):
    c = a * 4097.0
    h = c - (c - a)
    return h, a - h


def mul(a, b):
    p = a[0] * b[0]
    ah, al = split(a[0])
    bh, bl = split(b[0])
    e = ((ah * bh - p) + ah * bl + al * bh) + al * bl
    return quick(p, e + (a[0] * b[1] + a[1] * b[0]))


def add(a, b):
    s, e = two_sum(a[0], b[0])
    return quick(s, e + (a[1] + b[1]))


def neg(a):
    return -a[0], -a[1]


def sub(a, b):
    return add(a, neg(b))


def div(a, b):
    q = a[0] / b[0]
    r = sub(a, mul((q, jnp.zeros_like(q)), b))
    return quick(q, r[0] / b[0])


def clamp(a):
    inside = (a[0] >= LOW) & (a[0] <= HIGH)
    edge = jnp.where(a[0] < LOW, LOW, HIGH)
    return jnp.where(inside, a[0], edge), jnp.where(inside, a[1], 0.0)


def nonneg(a):
    keep = a[0] > 0.0
    return jnp.where(keep, a[0], 0.0), jnp.where(keep, a[1], 0.0)


def quadrature(shifts_all, shape):
    lane = lax.broadcasted_iota(jnp.int32, shape, 1)
    spacing = 10.0 / shifts_all
    coef = 2.0 * spacing * math.sin(math.pi * FRACTION) / math.pi
    node = spacing * (jnp.minimum(lane, shifts_all - 1).astype(jnp.float32) - shifts_all / 2 + 0.5)
    weight = jnp.where(lane < shifts_all, coef * jnp.exp((1.0 - FRACTION) * node), 0.0)
    sigma = jnp.exp(node)
    return sigma, weight


def coefficients(m, sigma, weight):
    one = jnp.ones_like(m[0][0])
    a0 = clamp(div(m[1], m[0]))
    g1 = nonneg(sub(m[2], mul(a0, m[1])))
    h1 = add(sub(m[3], mul((2.0 * a0[0], 2.0 * a0[1]), m[2])), mul(mul(a0, a0), m[1]))
    some1 = g1[0] > 0.0
    g1s = jnp.where(some1, g1[0], one), jnp.where(some1, g1[1], 0.0)
    a1 = clamp(div(h1, g1s))
    b1 = nonneg(div(g1, m[0]))
    s = neg(add(a0, a1))
    t = sub(mul(a0, a1), b1)
    r3 = add(m[4], add(mul(s, m[3]), mul(t, m[2])))
    g2 = nonneg(r3)
    h2 = add(add(m[5], mul(s, m[4])), add(mul(t, m[3]), mul(s, r3)))
    some2 = g2[0] > 0.0
    g2s = jnp.where(some2, g2[0], one)
    a0, a1, b1, t, s = a0[0], a1[0], b1[0], t[0], s[0]
    a2 = jnp.clip(h2[0] / g2s, LOW, HIGH)
    b1 = jnp.minimum(b1, jnp.maximum((HIGH - a0) * (a0 - LOW), 0.0))
    b2 = jnp.minimum(g2[0] / g1s[0], jnp.maximum((HIGH - a1) * (a1 - LOW), 0.0))

    d2 = sigma + a2
    d1 = jnp.maximum((sigma + a1) - b2 / d2, sigma + LOW)
    d0 = jnp.maximum((sigma + a0) - b1 / d1, sigma + LOW)
    y0 = weight / d0
    y1 = -y0 / d1
    y2 = -y1 / d2
    y0, y1, y2 = (jnp.sum(y, axis=1, keepdims=True) for y in (y0, y1, y2))
    a0, s, t = a0[:, :1], s[:, :1], t[:, :1]
    return y0 - a0 * y1 + t * y2, y1 + s * y2, y2


def kernel(
    n_space, n_shift, column, state, reaction, out,
    bb, rr, v1, v2, u0, w0, p0, recv_b, recv_u, recv_p, recv_r, acc, tile, tiles, pair, pairs,
    load_b, load_r, send_x, got_b, got_u, got_p, got_r, send_1, got_1, send_2, got_2,
):
    space, member = lax.axis_index("space"), lax.axis_index("shift")
    planes, rows, width = state.shape
    piece = rows // PIECES
    half = n_shift // 2
    high = member // half
    is_outer = (member % (n_shift - 1)) == 0
    outer = jnp.where(is_outer, 1, 0)
    depth = 2 * (1 - outer)

    def plane(k):
        return k + high * (planes - 1 - 2 * k)

    step = 2 * high - 1
    partner = (lax.rem(space + step + n_space, n_space), (n_shift - 1) * (1 - high))
    deep = column // n_shift
    chips = column // 2
    side = math.isqrt(n_space // deep)
    z, core = lax.rem(space, deep) * half + high, lax.rem(member, 2)
    y, x = space // deep // side, lax.rem(space // deep, side)

    def hops(distance, size):
        return min(distance, size - distance)

    up = sorted(
        ((dz, dc) for dz in range(chips) for dc in range(2) if dz + dc),
        key=lambda d: (-hops(d[0], chips), d))
    wide = sorted(
        ((dy, dx) for dy in range(side) for dx in range(side) if dy + dx),
        key=lambda d: (-hops(d[0], side) - hops(d[1], side), d))

    def beside(k):
        dz, dc = up[k]
        z2 = lax.rem(z + dz, chips)
        return space - lax.rem(space, deep) + z2 // half, lax.rem(z2, half) * 2 + lax.rem(core + dc, 2)

    def across(k):
        dy, dx = wide[k]
        chip = lax.rem(y + dy, side) * side + lax.rem(x + dx, side)
        return chip * deep + lax.rem(space, deep), member

    barrier = pltpu.get_barrier_semaphore()

    @pl.when(is_outer)
    def _():
        pl.semaphore_signal(barrier, inc=1, device_id=partner, device_id_type=MESH)

    for k in range(len(wide)):
        pl.semaphore_signal(barrier, inc=1, device_id=across(k), device_id_type=MESH)
    for k in range(len(up)):
        pl.semaphore_signal(barrier, inc=1, device_id=beside(k), device_id_type=MESH)

    def get_b(j):
        return pltpu.make_async_copy(
            state.at[plane(depth - 2 + j)], bb.at[j, pl.ds(PAD, rows)], load_b.at[j])

    def get_r(j):
        return pltpu.make_async_copy(reaction.at[plane(depth - 1 + j)], rr.at[j], load_r.at[j])

    def send_b(c, source=None):
        if source is None:
            source = state.at[plane(0), pl.ds(c * piece, piece)]
        return pltpu.make_async_remote_copy(
            src_ref=source, dst_ref=recv_b.at[c],
            send_sem=send_x.at[c], recv_sem=got_b.at[c],
            device_id=partner, device_id_type=MESH)

    def send_u(c):
        return pltpu.make_async_remote_copy(
            src_ref=u0.at[0, pl.ds(PAD + c * piece, piece)], dst_ref=recv_u.at[c],
            send_sem=send_x.at[PIECES + c], recv_sem=got_u.at[c],
            device_id=partner, device_id_type=MESH)

    def send_p(c):
        return pltpu.make_async_remote_copy(
            src_ref=p0.at[c], dst_ref=recv_p.at[c],
            send_sem=send_x.at[2 * PIECES + c], recv_sem=got_p.at[c],
            device_id=partner, device_id_type=MESH)

    def send_r(c):
        return pltpu.make_async_remote_copy(
            src_ref=reaction.at[plane(0), pl.ds(c * piece, piece)], dst_ref=recv_r.at[c],
            send_sem=send_x.at[3 * PIECES + c], recv_sem=got_r.at[c],
            device_id=partner, device_id_type=MESH)

    late_half = lax.rem(space, 2) == 1
    early_half = jnp.logical_not(late_half)
    from_late, from_early = range(PIECES - 1), range(PIECES - 1, PIECES)

    def loads():
        @pl.when(is_outer)
        def _():
            for j in range(2, 7):
                get_b(j).start()
            for j in range(1, 5):
                get_r(j).start()

        @pl.when(jnp.logical_not(is_outer))
        def _():
            for j in range(7):
                get_b(j).start()
            for j in range(5):
                get_r(j).start()

    acc[...] = jnp.zeros_like(acc)

    @pl.when(early_half)
    def _():
        loads()
        get_b(2).wait()

    pl.semaphore_wait(barrier, len(up) + len(wide) + outer)

    @pl.when(is_outer & early_half)
    def _():
        for c in range(PIECES):
            send_b(c, bb.at[2, pl.ds(PAD + c * piece, piece)]).start()

    @pl.when(late_half)
    def _():
        @pl.when(is_outer)
        def _():
            for c in range(PIECES):
                send_b(c).start()

        loads()
        get_b(2).wait()

    def wrap(ref, j):
        ref[j, PAD - 1 : PAD] = ref[j, PAD + rows - 1 : PAD + rows]
        ref[j, PAD + rows : PAD + rows + 1] = ref[j, PAD : PAD + 1]

    def at(ref, j, c, shift=0):
        return ref[j, pl.ds(PAD + c * piece + shift, piece)]

    def rows_of(c, start=0):
        first = c * piece + start
        return pl.ds(first if isinstance(c, int) else pl.multiple_of(first, 8), piece)

    def put(ref, j, c, value):
        ref[j, rows_of(c, PAD)] = value

    def coef_at(j, c):
        return rr[j, rows_of(c)] + 6.0

    def flat(ref, j, c):
        return ref[j, rows_of(c, PAD)]

    def applied(ref, j, c, r, sides):
        x = flat(ref, j, c)
        near = at(ref, j, c, -1) + at(ref, j, c, 1)
        near = near + pltpu.roll(x, 1, 1) + pltpu.roll(x, width - 1, 1)
        for side in sides:
            near = near + flat(ref, side, c)
        return coef_at(r, c) * x - near

    def gather(k, product):
        acc[k] += jnp.sum(product.reshape(piece // 8, 8, width), axis=0)

    def each(body):
        for c in range(PIECES):
            body(c)

    def make_v1(j, sides):
        each(lambda c: put(v1, j, c, applied(bb, j + 1, c, j, sides)))
        wrap(v1, j)

    def make_v2(k, sides):
        each(lambda c: put(v2, k, c, applied(v1, k + 1, c, k + 1, sides)))

    def early(j):
        def body(c):
            b, v = flat(bb, j, c), flat(v1, j - 1, c)
            gather(0, b * b)
            gather(1, b * v)
            gather(2, v * v)

        each(body)

    def late(k):
        def body(c):
            v, u = flat(v1, k + 1, c), flat(v2, k, c)
            gather(3, v * u)
            gather(4, u * u)

        each(body)

    def last(k, scale):
        def body(c):
            u = flat(v2, k, c)
            near = pltpu.roll(u, width - 1, 1) + at(v2, k, c, 1)
            near = near + scale * flat(v2, k + 1, c)
            gather(5, u * (coef_at(k + 1, c) * u - 2.0 * near))

        each(body)

    @pl.when(jnp.logical_not(is_outer))
    def _():
        for j in (0, 1, 3, 4, 5, 6):
            get_b(j).wait()
        for j in range(1, 6):
            wrap(bb, j)
        for j in range(5):
            get_r(j).wait()
        for j in range(5):
            make_v1(j, (j, j + 2))
        for k in range(3):
            make_v2(k, (k, k + 2))
        for k in range(2):
            wrap(v2, k)
            early(k + 2)
            late(k)
        last(0, 1.0)
        last(1, 0.5)

    @pl.when(is_outer)
    def _():
        for j in range(3, 7):
            get_b(j).wait()
        wrap(bb, 2)
        for j in range(1, 5):
            get_r(j).wait()
        for c in range(PIECES):
            put(u0, 0, c, applied(bb, 2, c, 1, (3,)))
            send_u(c).start()
        wrap(u0, 0)
        for j in range(3, 6):
            wrap(bb, j)
        make_v1(2, (2, 4))

        def own_p(c):
            p0[c] = applied(u0, 0, c, 1, ()) - flat(v1, 2, c)

        @pl.when(late_half)
        def _():
            for c in from_late:
                own_p(c)
                send_p(c).start()
                send_r(c).start()

        @pl.when(early_half)
        def _():
            for c in from_early:
                own_p(c)
                send_p(c).start()
                send_r(c).start()

        for j in range(3, 5):
            make_v1(j, (j, j + 2))
        make_v2(2, (2, 4))
        make_v2(1, (3,))
        early(3)
        for c in range(PIECES):
            send_b(c).wait_recv()
            b = flat(bb, 2, c)
            v = flat(u0, 0, c) - recv_b[c]
            put(v1, 1, c, v)
            gather(0, b * b)
            gather(1, b * v)
            gather(2, v * v)
        wrap(v1, 1)
        for c in range(PIECES):
            w0[c] = applied(v1, 1, c, 1, (2,))
        each(lambda c: put(v2, 1, c, flat(v2, 1, c) - flat(v1, 1, c)))
        wrap(v2, 1)
        late(1)
        last(1, 1.0)
        for c in range(PIECES):
            send_u(c).wait_recv()
            u = w0[c] - (recv_u[c] - flat(bb, 2, c))
            put(v2, 0, c, u)
            gather(3, flat(v1, 1, c) * u)
            gather(4, u * u)
        wrap(v2, 0)
        last(0, 1.0)

        def edge(c):
            send_p(c).wait_recv()
            send_r(c).wait_recv()
            b = flat(bb, 2, c)
            near = at(bb, 2, c, -1) + at(bb, 2, c, 1)
            near = near + pltpu.roll(b, 1, 1) + pltpu.roll(b, width - 1, 1)
            far = recv_p[c] - ((recv_r[c] + 6.0) * b - near) - flat(v1, 1, c)
            gather(5, -2.0 * flat(v2, 0, c) * far)

        @pl.when(early_half)
        def _():
            for c in from_late:
                edge(c)

        @pl.when(late_half)
        def _():
            for c in from_early:
                edge(c)

    lanes = width // 2
    hi = jnp.zeros((8, lanes), jnp.float32)
    lane = lax.broadcasted_iota(jnp.int32, hi.shape, 1)
    line = lax.broadcasted_iota(jnp.int32, hi.shape, 0)
    for k in range(6):
        row = acc[k]
        row = jnp.sum(row[:, :lanes] + row[:, lanes:], axis=0, keepdims=True)
        hi = jnp.where(line == k, row, hi)
    grid = 192.0 * jnp.max(jnp.abs(hi), axis=1, keepdims=True)
    coarse = (hi + grid) - grid
    hi, lo = two_sum(
        jnp.sum(coarse, axis=1, keepdims=True), jnp.sum(hi - coarse, axis=1, keepdims=True))
    packed = jnp.where(lane == line, hi, 0.0) + jnp.where(lane == line + 8, lo, 0.0)
    tile[...] = jnp.sum(packed, axis=0, keepdims=True)

    def merge(total, lost):
        return total + jnp.where(lane[:1] >= 8, pltpu.roll(lost, 8, 1), 0.0)

    def row_to(source, rows, k, send, got, to):
        return pltpu.make_async_remote_copy(
            src_ref=source, dst_ref=rows.at[k], send_sem=send, recv_sem=got,
            device_id=to, device_id_type=MESH)

    def all_rows(rows, send, got):
        return pltpu.make_async_remote_copy(
            src_ref=rows, dst_ref=rows, send_sem=send, recv_sem=got,
            device_id=across(0), device_id_type=MESH)

    def summed(own, rows):
        total, lost = own, jnp.zeros(own.shape, jnp.float32)
        for k in range(rows.shape[0]):
            total, e = two_sum(total, rows[k])
            lost = lost + e
        return merge(total, lost)

    for k in range(len(up)):
        row_to(tile, tiles, k, send_1, got_1, beside(k)).start()
    all_rows(tiles, send_1, got_1).wait_recv()
    pair[...] = summed(tile[...], tiles)
    for k in range(len(wide)):
        row_to(pair, pairs, k, send_2, got_2, across(k)).start()
    all_rows(tiles, send_1, got_1).wait_send()

    @pl.when(is_outer)
    def _():
        for c in range(PIECES):
            send_b(c).wait_send()
            send_u(c).wait_send()

        @pl.when(late_half)
        def _():
            for c in from_late:
                send_p(c).wait_send()
                send_r(c).wait_send()

        @pl.when(early_half)
        def _():
            for c in from_early:
                send_p(c).wait_send()
                send_r(c).wait_send()

    sigma, weight = quadrature(SH_DEV * n_shift, tile.shape)
    all_rows(pairs, send_2, got_2).wait_recv()
    total = summed(pair[...], pairs)
    total = jnp.broadcast_to(total, lane.shape)
    hi = jnp.sum(jnp.where(lane == line, total, 0.0), axis=1, keepdims=True)
    lo = jnp.sum(jnp.where(lane == line + 8, total, 0.0), axis=1, keepdims=True)
    hi, lo = jnp.broadcast_to(hi, lane.shape), jnp.broadcast_to(lo, lane.shape)
    hi, lo = quick(hi, lo)
    moments = [(hi[k : k + 1], lo[k : k + 1]) for k in range(6)]
    c0, c1, c2 = coefficients(moments, sigma, weight)

    for k in range(2):
        def body(c, k=k):
            value = c0 * flat(bb, k + 2, c) + c1 * flat(v1, k + 1, c) + c2 * flat(v2, k, c)
            out[k + high * (1 - 2 * k), rows_of(c)] = value

        each(body)
    all_rows(pairs, send_2, got_2).wait_send()


def on_device(state, reaction):
    n_space, n_shift = lax.axis_size("space"), lax.axis_size("shift")
    planes, rows, width = state.shape
    column = 2 * n_shift
    columns = n_space * n_shift // column
    piece = rows // PIECES
    f32 = jnp.float32
    padded = rows + 2 * PAD
    dma = pltpu.SemaphoreType.DMA
    cells = 2 * rows * width
    return pl.pallas_call(
        functools.partial(kernel, n_space, n_shift, column),
        out_shape=pltpu.VMEM((planes // n_shift, rows, width), f32),
        in_specs=[pl.BlockSpec(memory_space=pltpu.HBM)] * 2,
        out_specs=pl.BlockSpec(memory_space=pltpu.VMEM),
        scratch_shapes=[
            pltpu.VMEM((7, padded, width), f32),
            pltpu.VMEM((5, rows, width), f32),
            pltpu.VMEM((5, padded, width), f32),
            pltpu.VMEM((3, padded, width), f32),
            pltpu.VMEM((1, padded, width), f32),
            pltpu.VMEM((PIECES, piece, width), f32),
            pltpu.VMEM((PIECES, piece, width), f32),
            pltpu.VMEM((PIECES, piece, width), f32),
            pltpu.VMEM((PIECES, piece, width), f32),
            pltpu.VMEM((PIECES, piece, width), f32),
            pltpu.VMEM((PIECES, piece, width), f32),
            pltpu.VMEM((6, 8, width), f32),
            pltpu.VMEM((1, width // 2), f32),
            pltpu.VMEM((column - 1, 1, width // 2), f32),
            pltpu.VMEM((1, width // 2), f32),
            pltpu.VMEM((columns - 1, 1, width // 2), f32),
            dma((7,)),
            dma((5,)),
            dma((4 * PIECES,)),
            dma((PIECES,)),
            dma((PIECES,)),
            dma((PIECES,)),
            dma((PIECES,)),
            dma,
            dma,
            dma,
            dma,
        ],
        compiler_params=pltpu.CompilerParams(
            collective_id=0, has_side_effects=True, vmem_limit_bytes=58 * 2**20),
        cost_estimate=pl.CostEstimate(
            flops=100 * cells, bytes_accessed=40 * cells, transcendentals=0),
    )(state, reaction)


def solution(mesh):
    in_specs = (P("space", None, None), P("space", None, None))
    out_specs = P(("space", "shift"), None, None)
    return jax.shard_map(
        on_device, mesh=mesh, in_specs=in_specs, out_specs=out_specs, check_vma=False
    )
```

```python
import functools
import math

import jax
import jax.numpy as jnp
from jax import lax
from jax.experimental import pallas as pl
from jax.experimental.pallas import tpu as pltpu
from jax.sharding import PartitionSpec as P

MESH = pl.DeviceIdType.MESH
SH_DEV = 4
FRACTION = 0.4
LOW, HIGH = 0.05, 12.5
PIECES = 4
PAD = 8


def two_sum(a, b):
    s = a + b
    t = s - a
    return s, (a - (s - t)) + (b - t)


def quick(s, e):
    t = s + e
    return t, e - (t - s)


def split(a):
    c = a * 4097.0
    h = c - (c - a)
    return h, a - h


def mul(a, b):
    p = a[0] * b[0]
    ah, al = split(a[0])
    bh, bl = split(b[0])
    e = ((ah * bh - p) + ah * bl + al * bh) + al * bl
    return quick(p, e + (a[0] * b[1] + a[1] * b[0]))


def add(a, b):
    s, e = two_sum(a[0], b[0])
    return quick(s, e + (a[1] + b[1]))


def neg(a):
    return -a[0], -a[1]


def sub(a, b):
    return add(a, neg(b))


def div(a, b):
    q = a[0] / b[0]
    r = sub(a, mul((q, jnp.zeros_like(q)), b))
    return quick(q, r[0] / b[0])


def clamp(a):
    inside = (a[0] >= LOW) & (a[0] <= HIGH)
    edge = jnp.where(a[0] < LOW, LOW, HIGH)
    return jnp.where(inside, a[0], edge), jnp.where(inside, a[1], 0.0)


def nonneg(a):
    keep = a[0] > 0.0
    return jnp.where(keep, a[0], 0.0), jnp.where(keep, a[1], 0.0)


def quadrature(shifts_all, shape):
    lane = lax.broadcasted_iota(jnp.int32, shape, 1)
    spacing = 10.0 / shifts_all
    coef = 2.0 * spacing * math.sin(math.pi * FRACTION) / math.pi
    node = spacing * (jnp.minimum(lane, shifts_all - 1).astype(jnp.float32) - shifts_all / 2 + 0.5)
    weight = jnp.where(lane < shifts_all, coef * jnp.exp((1.0 - FRACTION) * node), 0.0)
    sigma = jnp.exp(node)
    return sigma, weight


def coefficients(m, sigma, weight):
    one = jnp.ones_like(m[0][0])
    a0 = clamp(div(m[1], m[0]))
    g1 = nonneg(sub(m[2], mul(a0, m[1])))
    h1 = add(sub(m[3], mul((2.0 * a0[0], 2.0 * a0[1]), m[2])), mul(mul(a0, a0), m[1]))
    some1 = g1[0] > 0.0
    g1s = jnp.where(some1, g1[0], one), jnp.where(some1, g1[1], 0.0)
    a1 = clamp(div(h1, g1s))
    b1 = nonneg(div(g1, m[0]))
    s = neg(add(a0, a1))
    t = sub(mul(a0, a1), b1)
    r3 = add(m[4], add(mul(s, m[3]), mul(t, m[2])))
    g2 = nonneg(r3)
    h2 = add(add(m[5], mul(s, m[4])), add(mul(t, m[3]), mul(s, r3)))
    some2 = g2[0] > 0.0
    g2s = jnp.where(some2, g2[0], one)
    a0, a1, b1, t, s = a0[0], a1[0], b1[0], t[0], s[0]
    a2 = jnp.clip(h2[0] / g2s, LOW, HIGH)
    b1 = jnp.minimum(b1, jnp.maximum((HIGH - a0) * (a0 - LOW), 0.0))
    b2 = jnp.minimum(g2[0] / g1s[0], jnp.maximum((HIGH - a1) * (a1 - LOW), 0.0))

    d2 = sigma + a2
    d1 = jnp.maximum((sigma + a1) - b2 / d2, sigma + LOW)
    d0 = jnp.maximum((sigma + a0) - b1 / d1, sigma + LOW)
    y0 = weight / d0
    y1 = -y0 / d1
    y2 = -y1 / d2
    y0, y1, y2 = (jnp.sum(y, axis=1, keepdims=True) for y in (y0, y1, y2))
    a0, s, t = a0[:, :1], s[:, :1], t[:, :1]
    return y0 - a0 * y1 + t * y2, y1 + s * y2, y2


def kernel(
    n_space, n_shift, column, state, reaction, out,
    bb, rr, v1, v2, u0, w0, p0, recv_b, recv_u, recv_p, recv_r, acc, tile, tiles, pair, pairs,
    load_b, load_r, send_x, got_b, got_u, got_p, got_r, send_1, got_1, send_2, got_2,
):
    space, member = lax.axis_index("space"), lax.axis_index("shift")
    planes, rows, width = state.shape
    piece = rows // PIECES
    half = n_shift // 2
    high = member // half
    is_outer = (member % (n_shift - 1)) == 0
    outer = jnp.where(is_outer, 1, 0)
    depth = 2 * (1 - outer)

    def plane(k):
        return k + high * (planes - 1 - 2 * k)

    step = 2 * high - 1
    partner = (lax.rem(space + step + n_space, n_space), (n_shift - 1) * (1 - high))
    deep = column // n_shift
    chips = column // 2
    side = math.isqrt(n_space // deep)
    z, core = lax.rem(space, deep) * half + high, lax.rem(member, 2)
    y, x = space // deep // side, lax.rem(space // deep, side)

    def hops(distance, size):
        return min(distance, size - distance)

    up = sorted(
        ((dz, dc) for dz in range(chips) for dc in range(2) if dz + dc),
        key=lambda d: (-hops(d[0], chips), d))
    wide = sorted(
        ((dy, dx) for dy in range(side) for dx in range(side) if dy + dx),
        key=lambda d: (-hops(d[0], side) - hops(d[1], side), d))

    def beside(k):
        dz, dc = up[k]
        z2 = lax.rem(z + dz, chips)
        return space - lax.rem(space, deep) + z2 // half, lax.rem(z2, half) * 2 + lax.rem(core + dc, 2)

    def across(k):
        dy, dx = wide[k]
        chip = lax.rem(y + dy, side) * side + lax.rem(x + dx, side)
        return chip * deep + lax.rem(space, deep), member

    barrier = pltpu.get_barrier_semaphore()

    @pl.when(is_outer)
    def _():
        pl.semaphore_signal(barrier, inc=1, device_id=partner, device_id_type=MESH)

    for k in range(len(wide)):
        pl.semaphore_signal(barrier, inc=1, device_id=across(k), device_id_type=MESH)
    for k in range(len(up)):
        pl.semaphore_signal(barrier, inc=1, device_id=beside(k), device_id_type=MESH)

    def get_b(j):
        return pltpu.make_async_copy(
            state.at[plane(depth - 2 + j)], bb.at[j, pl.ds(PAD, rows)], load_b.at[j])

    def get_r(j):
        return pltpu.make_async_copy(reaction.at[plane(depth - 1 + j)], rr.at[j], load_r.at[j])

    def send_b(c, source=None):
        if source is None:
            source = state.at[plane(0), pl.ds(c * piece, piece)]
        return pltpu.make_async_remote_copy(
            src_ref=source, dst_ref=recv_b.at[c],
            send_sem=send_x.at[c], recv_sem=got_b.at[c],
            device_id=partner, device_id_type=MESH)

    def send_u(c):
        return pltpu.make_async_remote_copy(
            src_ref=u0.at[0, pl.ds(PAD + c * piece, piece)], dst_ref=recv_u.at[c],
            send_sem=send_x.at[PIECES + c], recv_sem=got_u.at[c],
            device_id=partner, device_id_type=MESH)

    def send_p(c):
        return pltpu.make_async_remote_copy(
            src_ref=p0.at[c], dst_ref=recv_p.at[c],
            send_sem=send_x.at[2 * PIECES + c], recv_sem=got_p.at[c],
            device_id=partner, device_id_type=MESH)

    def send_w(c):
        return pltpu.make_async_remote_copy(
            src_ref=w0.at[c], dst_ref=recv_p.at[c],
            send_sem=send_x.at[2 * PIECES + c], recv_sem=got_p.at[c],
            device_id=partner, device_id_type=MESH)

    def send_r(c):
        return pltpu.make_async_remote_copy(
            src_ref=reaction.at[plane(0), pl.ds(c * piece, piece)], dst_ref=recv_r.at[c],
            send_sem=send_x.at[3 * PIECES + c], recv_sem=got_r.at[c],
            device_id=partner, device_id_type=MESH)

    late_half = lax.rem(space, 2) == 1
    early_half = jnp.logical_not(late_half)
    from_late, from_early = range(PIECES - 1), range(PIECES - 1, PIECES)

    def loads():
        @pl.when(is_outer)
        def _():
            for j in range(2, 7):
                get_b(j).start()
            for j in range(1, 5):
                get_r(j).start()

        @pl.when(jnp.logical_not(is_outer))
        def _():
            for j in range(7):
                get_b(j).start()
            for j in range(5):
                get_r(j).start()

    acc[...] = jnp.zeros_like(acc)

    @pl.when(early_half)
    def _():
        loads()
        get_b(2).wait()

    pl.semaphore_wait(barrier, len(up) + len(wide) + outer)

    @pl.when(is_outer & early_half)
    def _():
        for c in range(PIECES):
            send_b(c, bb.at[2, pl.ds(PAD + c * piece, piece)]).start()

    @pl.when(late_half)
    def _():
        @pl.when(is_outer)
        def _():
            for c in range(PIECES):
                send_b(c).start()

        loads()
        get_b(2).wait()

    def wrap(ref, j):
        ref[j, PAD - 1 : PAD] = ref[j, PAD + rows - 1 : PAD + rows]
        ref[j, PAD + rows : PAD + rows + 1] = ref[j, PAD : PAD + 1]

    def at(ref, j, c, shift=0):
        return ref[j, pl.ds(PAD + c * piece + shift, piece)]

    def rows_of(c, start=0):
        first = c * piece + start
        return pl.ds(first if isinstance(c, int) else pl.multiple_of(first, 8), piece)

    def put(ref, j, c, value):
        ref[j, rows_of(c, PAD)] = value

    def coef_at(j, c):
        return rr[j, rows_of(c)] + 6.0

    def flat(ref, j, c):
        return ref[j, rows_of(c, PAD)]

    def applied(ref, j, c, r, sides):
        x = flat(ref, j, c)
        near = at(ref, j, c, -1) + at(ref, j, c, 1)
        near = near + pltpu.roll(x, 1, 1) + pltpu.roll(x, width - 1, 1)
        for side in sides:
            near = near + flat(ref, side, c)
        return coef_at(r, c) * x - near

    def gather(k, product):
        acc[k] += jnp.sum(product.reshape(piece // 8, 8, width), axis=0)

    def each(body):
        for c in range(PIECES):
            body(c)

    def make_v1(j, sides):
        each(lambda c: put(v1, j, c, applied(bb, j + 1, c, j, sides)))
        wrap(v1, j)

    def make_v2(k, sides):
        each(lambda c: put(v2, k, c, applied(v1, k + 1, c, k + 1, sides)))

    def early(j):
        def body(c):
            b, v = flat(bb, j, c), flat(v1, j - 1, c)
            gather(0, b * b)
            gather(1, b * v)
            gather(2, v * v)

        each(body)

    def late(k):
        def body(c):
            v, u = flat(v1, k + 1, c), flat(v2, k, c)
            gather(3, v * u)
            gather(4, u * u)

        each(body)

    def last(k, scale):
        def body(c):
            u = flat(v2, k, c)
            near = pltpu.roll(u, width - 1, 1) + at(v2, k, c, 1)
            near = near + scale * flat(v2, k + 1, c)
            gather(5, u * (coef_at(k + 1, c) * u - 2.0 * near))

        each(body)

    @pl.when(jnp.logical_not(is_outer))
    def _():
        for j in (0, 1, 3, 4, 5, 6):
            get_b(j).wait()
        for j in range(1, 6):
            wrap(bb, j)
        for j in range(5):
            get_r(j).wait()
        for j in range(5):
            make_v1(j, (j, j + 2))
        for k in range(3):
            make_v2(k, (k, k + 2))
        for k in range(2):
            wrap(v2, k)
            early(k + 2)
            late(k)
        last(0, 1.0)
        last(1, 0.5)

    @pl.when(is_outer)
    def _():
        for j in range(3, 7):
            get_b(j).wait()
        wrap(bb, 2)
        for j in range(1, 5):
            get_r(j).wait()
        for c in range(PIECES):
            put(u0, 0, c, applied(bb, 2, c, 1, (3,)))
            send_u(c).start()
        wrap(u0, 0)
        for j in range(3, 6):
            wrap(bb, j)
        make_v1(2, (2, 4))

        def own_p(c):
            p0[c] = applied(u0, 0, c, 1, ()) - flat(v1, 2, c)

        @pl.when(late_half)
        def _():
            for c in from_late:
                own_p(c)
                send_p(c).start()
                send_r(c).start()

        for j in range(3, 5):
            make_v1(j, (j, j + 2))
        make_v2(2, (2, 4))
        make_v2(1, (3,))
        early(3)
        for c in range(PIECES):
            send_b(c).wait_recv()
            b = flat(bb, 2, c)
            v = flat(u0, 0, c) - recv_b[c]
            put(v1, 1, c, v)
            gather(0, b * b)
            gather(1, b * v)
            gather(2, v * v)
        wrap(v1, 1)
        def own_w(c):
            w0[c] = applied(v1, 1, c, 1, (2,))

        for c in from_early:
            own_w(c)

        @pl.when(early_half)
        def _():
            for c in from_early:
                send_w(c).start()

        for c in from_late:
            own_w(c)
        each(lambda c: put(v2, 1, c, flat(v2, 1, c) - flat(v1, 1, c)))
        wrap(v2, 1)
        late(1)
        last(1, 1.0)
        for c in range(PIECES):
            send_u(c).wait_recv()
            u = w0[c] - (recv_u[c] - flat(bb, 2, c))
            put(v2, 0, c, u)
            gather(3, flat(v1, 1, c) * u)
            gather(4, u * u)
        wrap(v2, 0)
        last(0, 1.0)

        def edge(c):
            send_p(c).wait_recv()
            send_r(c).wait_recv()
            b = flat(bb, 2, c)
            near = at(bb, 2, c, -1) + at(bb, 2, c, 1)
            near = near + pltpu.roll(b, 1, 1) + pltpu.roll(b, width - 1, 1)
            far = recv_p[c] - ((recv_r[c] + 6.0) * b - near) - flat(v1, 1, c)
            gather(5, -2.0 * flat(v2, 0, c) * far)

        @pl.when(early_half)
        def _():
            for c in from_late:
                edge(c)

        @pl.when(late_half)
        def _():
            for c in from_early:
                send_w(c).wait_recv()
                gather(5, -2.0 * flat(v2, 0, c) * (recv_p[c] - flat(v1, 1, c)))

    lanes = width // 2
    hi = jnp.zeros((8, lanes), jnp.float32)
    lane = lax.broadcasted_iota(jnp.int32, hi.shape, 1)
    line = lax.broadcasted_iota(jnp.int32, hi.shape, 0)
    for k in range(6):
        row = acc[k]
        row = jnp.sum(row[:, :lanes] + row[:, lanes:], axis=0, keepdims=True)
        hi = jnp.where(line == k, row, hi)
    grid = 192.0 * jnp.max(jnp.abs(hi), axis=1, keepdims=True)
    coarse = (hi + grid) - grid
    hi, lo = two_sum(
        jnp.sum(coarse, axis=1, keepdims=True), jnp.sum(hi - coarse, axis=1, keepdims=True))
    packed = jnp.where(lane == line, hi, 0.0) + jnp.where(lane == line + 8, lo, 0.0)
    tile[...] = jnp.sum(packed, axis=0, keepdims=True)

    def merge(total, lost):
        return total + jnp.where(lane[:1] >= 8, pltpu.roll(lost, 8, 1), 0.0)

    def row_to(source, rows, k, send, got, to):
        return pltpu.make_async_remote_copy(
            src_ref=source, dst_ref=rows.at[k], send_sem=send, recv_sem=got,
            device_id=to, device_id_type=MESH)

    def all_rows(rows, send, got):
        return pltpu.make_async_remote_copy(
            src_ref=rows, dst_ref=rows, send_sem=send, recv_sem=got,
            device_id=across(0), device_id_type=MESH)

    def summed(own, rows):
        total, lost = own, jnp.zeros(own.shape, jnp.float32)
        for k in range(rows.shape[0]):
            total, e = two_sum(total, rows[k])
            lost = lost + e
        return merge(total, lost)

    for k in range(len(up)):
        row_to(tile, tiles, k, send_1, got_1, beside(k)).start()
    all_rows(tiles, send_1, got_1).wait_recv()
    pair[...] = summed(tile[...], tiles)
    for k in range(len(wide)):
        row_to(pair, pairs, k, send_2, got_2, across(k)).start()
    all_rows(tiles, send_1, got_1).wait_send()

    @pl.when(is_outer)
    def _():
        for c in range(PIECES):
            send_b(c).wait_send()
            send_u(c).wait_send()

        @pl.when(late_half)
        def _():
            for c in from_late:
                send_p(c).wait_send()
                send_r(c).wait_send()

        @pl.when(early_half)
        def _():
            for c in from_early:
                send_w(c).wait_send()

    sigma, weight = quadrature(SH_DEV * n_shift, tile.shape)
    all_rows(pairs, send_2, got_2).wait_recv()
    total = summed(pair[...], pairs)
    total = jnp.broadcast_to(total, lane.shape)
    hi = jnp.sum(jnp.where(lane == line, total, 0.0), axis=1, keepdims=True)
    lo = jnp.sum(jnp.where(lane == line + 8, total, 0.0), axis=1, keepdims=True)
    hi, lo = jnp.broadcast_to(hi, lane.shape), jnp.broadcast_to(lo, lane.shape)
    hi, lo = quick(hi, lo)
    moments = [(hi[k : k + 1], lo[k : k + 1]) for k in range(6)]
    c0, c1, c2 = coefficients(moments, sigma, weight)

    for k in range(2):
        def body(c, k=k):
            value = c0 * flat(bb, k + 2, c) + c1 * flat(v1, k + 1, c) + c2 * flat(v2, k, c)
            out[k + high * (1 - 2 * k), rows_of(c)] = value

        each(body)
    all_rows(pairs, send_2, got_2).wait_send()


def on_device(state, reaction):
    n_space, n_shift = lax.axis_size("space"), lax.axis_size("shift")
    planes, rows, width = state.shape
    column = 2 * n_shift
    columns = n_space * n_shift // column
    piece = rows // PIECES
    f32 = jnp.float32
    padded = rows + 2 * PAD
    dma = pltpu.SemaphoreType.DMA
    cells = 2 * rows * width
    return pl.pallas_call(
        functools.partial(kernel, n_space, n_shift, column),
        out_shape=pltpu.VMEM((planes // n_shift, rows, width), f32),
        in_specs=[pl.BlockSpec(memory_space=pltpu.HBM)] * 2,
        out_specs=pl.BlockSpec(memory_space=pltpu.VMEM),
        scratch_shapes=[
            pltpu.VMEM((7, padded, width), f32),
            pltpu.VMEM((5, rows, width), f32),
            pltpu.VMEM((5, padded, width), f32),
            pltpu.VMEM((3, padded, width), f32),
            pltpu.VMEM((1, padded, width), f32),
            pltpu.VMEM((PIECES, piece, width), f32),
            pltpu.VMEM((PIECES, piece, width), f32),
            pltpu.VMEM((PIECES, piece, width), f32),
            pltpu.VMEM((PIECES, piece, width), f32),
            pltpu.VMEM((PIECES, piece, width), f32),
            pltpu.VMEM((PIECES, piece, width), f32),
            pltpu.VMEM((6, 8, width), f32),
            pltpu.VMEM((1, width // 2), f32),
            pltpu.VMEM((column - 1, 1, width // 2), f32),
            pltpu.VMEM((1, width // 2), f32),
            pltpu.VMEM((columns - 1, 1, width // 2), f32),
            dma((7,)),
            dma((5,)),
            dma((4 * PIECES,)),
            dma((PIECES,)),
            dma((PIECES,)),
            dma((PIECES,)),
            dma((PIECES,)),
            dma,
            dma,
            dma,
            dma,
        ],
        compiler_params=pltpu.CompilerParams(
            collective_id=0, has_side_effects=True, vmem_limit_bytes=58 * 2**20),
        cost_estimate=pl.CostEstimate(
            flops=100 * cells, bytes_accessed=40 * cells, transcendentals=0),
    )(state, reaction)


def solution(mesh):
    in_specs = (P("space", None, None), P("space", None, None))
    out_specs = P(("space", "shift"), None, None)
    return jax.shard_map(
        on_device, mesh=mesh, in_specs=in_specs, out_specs=out_specs, check_vma=False
    )
```

```python
import functools
import math

import jax
import jax.numpy as jnp
from jax import lax
from jax.experimental import pallas as pl
from jax.experimental.pallas import tpu as pltpu
from jax.sharding import PartitionSpec as P

MESH = pl.DeviceIdType.MESH
SH_DEV = 4
FRACTION = 0.4
LOW, HIGH = 0.05, 12.5
PIECES = 4
PAD = 8


def two_sum(a, b):
    s = a + b
    t = s - a
    return s, (a - (s - t)) + (b - t)


def quick(s, e):
    t = s + e
    return t, e - (t - s)


def split(a):
    c = a * 4097.0
    h = c - (c - a)
    return h, a - h


def mul(a, b):
    p = a[0] * b[0]
    ah, al = split(a[0])
    bh, bl = split(b[0])
    e = ((ah * bh - p) + ah * bl + al * bh) + al * bl
    return quick(p, e + (a[0] * b[1] + a[1] * b[0]))


def add(a, b):
    s, e = two_sum(a[0], b[0])
    return quick(s, e + (a[1] + b[1]))


def neg(a):
    return -a[0], -a[1]


def sub(a, b):
    return add(a, neg(b))


def div(a, b):
    q = a[0] / b[0]
    r = sub(a, mul((q, jnp.zeros_like(q)), b))
    return quick(q, r[0] / b[0])


def clamp(a):
    inside = (a[0] >= LOW) & (a[0] <= HIGH)
    edge = jnp.where(a[0] < LOW, LOW, HIGH)
    return jnp.where(inside, a[0], edge), jnp.where(inside, a[1], 0.0)


def nonneg(a):
    keep = a[0] > 0.0
    return jnp.where(keep, a[0], 0.0), jnp.where(keep, a[1], 0.0)


def quadrature(shifts_all, shape):
    lane = lax.broadcasted_iota(jnp.int32, shape, 1)
    spacing = 10.0 / shifts_all
    coef = 2.0 * spacing * math.sin(math.pi * FRACTION) / math.pi
    node = spacing * (jnp.minimum(lane, shifts_all - 1).astype(jnp.float32) - shifts_all / 2 + 0.5)
    weight = jnp.where(lane < shifts_all, coef * jnp.exp((1.0 - FRACTION) * node), 0.0)
    sigma = jnp.exp(node)
    return sigma, weight


def coefficients(m, sigma, weight):
    one = jnp.ones_like(m[0][0])
    a0 = clamp(div(m[1], m[0]))
    g1 = nonneg(sub(m[2], mul(a0, m[1])))
    h1 = add(sub(m[3], mul((2.0 * a0[0], 2.0 * a0[1]), m[2])), mul(mul(a0, a0), m[1]))
    some1 = g1[0] > 0.0
    g1s = jnp.where(some1, g1[0], one), jnp.where(some1, g1[1], 0.0)
    a1 = clamp(div(h1, g1s))
    b1 = nonneg(div(g1, m[0]))
    s = neg(add(a0, a1))
    t = sub(mul(a0, a1), b1)
    r3 = add(m[4], add(mul(s, m[3]), mul(t, m[2])))
    g2 = nonneg(r3)
    h2 = add(add(m[5], mul(s, m[4])), add(mul(t, m[3]), mul(s, r3)))
    some2 = g2[0] > 0.0
    g2s = jnp.where(some2, g2[0], one)
    a0, a1, b1, t, s = a0[0], a1[0], b1[0], t[0], s[0]
    a2 = jnp.clip(h2[0] / g2s, LOW, HIGH)
    b1 = jnp.minimum(b1, jnp.maximum((HIGH - a0) * (a0 - LOW), 0.0))
    b2 = jnp.minimum(g2[0] / g1s[0], jnp.maximum((HIGH - a1) * (a1 - LOW), 0.0))

    d2 = sigma + a2
    d1 = jnp.maximum((sigma + a1) - b2 / d2, sigma + LOW)
    d0 = jnp.maximum((sigma + a0) - b1 / d1, sigma + LOW)
    y0 = weight / d0
    y1 = -y0 / d1
    y2 = -y1 / d2
    y0, y1, y2 = (jnp.sum(y, axis=1, keepdims=True) for y in (y0, y1, y2))
    a0, s, t = a0[:, :1], s[:, :1], t[:, :1]
    return y0 - a0 * y1 + t * y2, y1 + s * y2, y2


def kernel(
    n_space, n_shift, column, state, reaction, out,
    bb, rr, v1, v2, u0, w0, p0, recv_b, recv_u, recv_p, recv_r, acc, tile, tiles, pair, pairs,
    load_b, load_r, send_x, got_b, got_u, got_p, got_r, send_1, got_1, send_2, got_2,
):
    space, member = lax.axis_index("space"), lax.axis_index("shift")
    planes, rows, width = state.shape
    piece = rows // PIECES
    half = n_shift // 2
    high = member // half
    is_outer = (member % (n_shift - 1)) == 0
    outer = jnp.where(is_outer, 1, 0)
    depth = 2 * (1 - outer)

    def plane(k):
        return k + high * (planes - 1 - 2 * k)

    step = 2 * high - 1
    partner = (lax.rem(space + step + n_space, n_space), (n_shift - 1) * (1 - high))
    deep = column // n_shift
    chips = column // 2
    side = math.isqrt(n_space // deep)
    z, core = lax.rem(space, deep) * half + high, lax.rem(member, 2)
    y, x = space // deep // side, lax.rem(space // deep, side)

    def hops(distance, size):
        return min(distance, size - distance)

    up = sorted(
        ((dz, dc) for dz in range(chips) for dc in range(2) if dz + dc),
        key=lambda d: (-hops(d[0], chips), d))
    wide = sorted(
        ((dy, dx) for dy in range(side) for dx in range(side) if dy + dx),
        key=lambda d: (-hops(d[0], side) - hops(d[1], side), d))

    def beside(k):
        dz, dc = up[k]
        z2 = lax.rem(z + dz, chips)
        return space - lax.rem(space, deep) + z2 // half, lax.rem(z2, half) * 2 + lax.rem(core + dc, 2)

    def across(k):
        dy, dx = wide[k]
        chip = lax.rem(y + dy, side) * side + lax.rem(x + dx, side)
        return chip * deep + lax.rem(space, deep), member

    barrier = pltpu.get_barrier_semaphore()

    @pl.when(is_outer)
    def _():
        pl.semaphore_signal(barrier, inc=1, device_id=partner, device_id_type=MESH)

    for k in range(len(wide)):
        pl.semaphore_signal(barrier, inc=1, device_id=across(k), device_id_type=MESH)
    for k in range(len(up)):
        pl.semaphore_signal(barrier, inc=1, device_id=beside(k), device_id_type=MESH)

    def get_b(j):
        return pltpu.make_async_copy(
            state.at[plane(depth - 2 + j)], bb.at[j, pl.ds(PAD, rows)], load_b.at[j])

    def get_r(j):
        return pltpu.make_async_copy(reaction.at[plane(depth - 1 + j)], rr.at[j], load_r.at[j])

    def send_b(c, source=None):
        if source is None:
            source = state.at[plane(0), pl.ds(c * piece, piece)]
        return pltpu.make_async_remote_copy(
            src_ref=source, dst_ref=recv_b.at[c],
            send_sem=send_x.at[c], recv_sem=got_b.at[c],
            device_id=partner, device_id_type=MESH)

    def send_u(c):
        return pltpu.make_async_remote_copy(
            src_ref=u0.at[0, pl.ds(PAD + c * piece, piece)], dst_ref=recv_u.at[c],
            send_sem=send_x.at[PIECES + c], recv_sem=got_u.at[c],
            device_id=partner, device_id_type=MESH)

    def send_p(c):
        return pltpu.make_async_remote_copy(
            src_ref=p0.at[c], dst_ref=recv_p.at[c],
            send_sem=send_x.at[2 * PIECES + c], recv_sem=got_p.at[c],
            device_id=partner, device_id_type=MESH)

    def send_w(c):
        return pltpu.make_async_remote_copy(
            src_ref=w0.at[c], dst_ref=recv_p.at[c],
            send_sem=send_x.at[2 * PIECES + c], recv_sem=got_p.at[c],
            device_id=partner, device_id_type=MESH)

    def send_r(c):
        return pltpu.make_async_remote_copy(
            src_ref=reaction.at[plane(0), pl.ds(c * piece, piece)], dst_ref=recv_r.at[c],
            send_sem=send_x.at[3 * PIECES + c], recv_sem=got_r.at[c],
            device_id=partner, device_id_type=MESH)

    late_half = lax.rem(space, 2) == 1
    early_half = jnp.logical_not(late_half)
    from_late, from_early = range(PIECES - 1), range(PIECES - 1, PIECES)

    def loads():
        @pl.when(is_outer)
        def _():
            for j in range(2, 7):
                get_b(j).start()
            for j in range(1, 5):
                get_r(j).start()

        @pl.when(jnp.logical_not(is_outer))
        def _():
            for j in range(7):
                get_b(j).start()
            for j in range(5):
                get_r(j).start()

    acc[...] = jnp.zeros_like(acc)

    @pl.when(early_half)
    def _():
        loads()
        get_b(2).wait()

    pl.semaphore_wait(barrier, len(up) + len(wide) + outer)

    @pl.when(is_outer & early_half)
    def _():
        for c in range(PIECES):
            send_b(c, bb.at[2, pl.ds(PAD + c * piece, piece)]).start()

    @pl.when(late_half)
    def _():
        @pl.when(is_outer)
        def _():
            for c in range(PIECES):
                send_b(c).start()

        loads()
        get_b(2).wait()

    def wrap(ref, j):
        ref[j, PAD - 1 : PAD] = ref[j, PAD + rows - 1 : PAD + rows]
        ref[j, PAD + rows : PAD + rows + 1] = ref[j, PAD : PAD + 1]

    def at(ref, j, c, shift=0):
        return ref[j, pl.ds(PAD + c * piece + shift, piece)]

    def rows_of(c, start=0):
        first = c * piece + start
        return pl.ds(first if isinstance(c, int) else pl.multiple_of(first, 8), piece)

    def put(ref, j, c, value):
        ref[j, rows_of(c, PAD)] = value

    def coef_at(j, c):
        return rr[j, rows_of(c)] + 6.0

    def flat(ref, j, c):
        return ref[j, rows_of(c, PAD)]

    def applied(ref, j, c, r, sides):
        x = flat(ref, j, c)
        near = at(ref, j, c, -1) + at(ref, j, c, 1)
        near = near + pltpu.roll(x, 1, 1) + pltpu.roll(x, width - 1, 1)
        for side in sides:
            near = near + flat(ref, side, c)
        return coef_at(r, c) * x - near

    def gather(k, product):
        acc[k] += jnp.sum(product.reshape(piece // 8, 8, width), axis=0)

    def each(body):
        for c in range(PIECES):
            body(c)

    def make_v1(j, sides):
        each(lambda c: put(v1, j, c, applied(bb, j + 1, c, j, sides)))
        wrap(v1, j)

    def make_v2(k, sides):
        each(lambda c: put(v2, k, c, applied(v1, k + 1, c, k + 1, sides)))

    def early(j):
        def body(c):
            b, v = flat(bb, j, c), flat(v1, j - 1, c)
            gather(0, b * b)
            gather(1, b * v)
            gather(2, v * v)

        each(body)

    def late(k):
        def body(c):
            v, u = flat(v1, k + 1, c), flat(v2, k, c)
            gather(3, v * u)
            gather(4, u * u)

        each(body)

    def last(k, scale):
        def body(c):
            u = flat(v2, k, c)
            near = pltpu.roll(u, width - 1, 1) + at(v2, k, c, 1)
            near = near + scale * flat(v2, k + 1, c)
            gather(5, u * (coef_at(k + 1, c) * u - 2.0 * near))

        each(body)

    @pl.when(jnp.logical_not(is_outer))
    def _():
        for j in (0, 1, 3, 4, 5, 6):
            get_b(j).wait()
        for j in range(1, 6):
            wrap(bb, j)
        for j in range(5):
            get_r(j).wait()
        for j in range(5):
            make_v1(j, (j, j + 2))
        for k in range(3):
            make_v2(k, (k, k + 2))
        for k in range(2):
            wrap(v2, k)
            early(k + 2)
            late(k)
        last(0, 1.0)
        last(1, 0.5)

    @pl.when(is_outer)
    def _():
        for j in range(3, 7):
            get_b(j).wait()
        wrap(bb, 2)
        for j in range(1, 5):
            get_r(j).wait()
        for c in range(PIECES):
            put(u0, 0, c, applied(bb, 2, c, 1, (3,)))
            send_u(c).start()
        wrap(u0, 0)
        for j in range(3, 6):
            wrap(bb, j)
        make_v1(2, (2, 4))

        def own_p(c):
            p0[c] = applied(u0, 0, c, 1, ()) - flat(v1, 2, c)

        @pl.when(late_half)
        def _():
            for c in from_late:
                own_p(c)
                send_p(c).start()
                send_r(c).start()

        for j in range(3, 5):
            make_v1(j, (j, j + 2))
        make_v2(2, (2, 4))
        make_v2(1, (3,))
        early(3)
        for c in range(PIECES):
            send_b(c).wait_recv()
            b = flat(bb, 2, c)
            v = flat(u0, 0, c) - recv_b[c]
            put(v1, 1, c, v)
            gather(0, b * b)
            gather(1, b * v)
            gather(2, v * v)
        wrap(v1, 1)
        def own_w(c):
            w0[c] = applied(v1, 1, c, 1, (2,))

        for c in from_early:
            own_w(c)

        @pl.when(early_half)
        def _():
            for c in from_early:
                send_w(c).start()

        for c in from_late:
            own_w(c)
        each(lambda c: put(v2, 1, c, flat(v2, 1, c) - flat(v1, 1, c)))
        wrap(v2, 1)
        late(1)
        last(1, 1.0)
        for c in range(PIECES):
            send_u(c).wait_recv()
            u = w0[c] - (recv_u[c] - flat(bb, 2, c))
            put(v2, 0, c, u)
            gather(3, flat(v1, 1, c) * u)
            gather(4, u * u)
        wrap(v2, 0)
        last(0, 1.0)

        def edge(c):
            send_p(c).wait_recv()
            send_r(c).wait_recv()
            b = flat(bb, 2, c)
            near = at(bb, 2, c, -1) + at(bb, 2, c, 1)
            near = near + pltpu.roll(b, 1, 1) + pltpu.roll(b, width - 1, 1)
            far = recv_p[c] - ((recv_r[c] + 6.0) * b - near) - flat(v1, 1, c)
            gather(5, -2.0 * flat(v2, 0, c) * far)

        @pl.when(early_half)
        def _():
            for c in from_late:
                edge(c)

        @pl.when(late_half)
        def _():
            for c in from_early:
                send_w(c).wait_recv()
                gather(5, -2.0 * flat(v2, 0, c) * (recv_p[c] - flat(v1, 1, c)))

    lanes = width // 2
    hi = jnp.zeros((8, lanes), jnp.float32)
    lane = lax.broadcasted_iota(jnp.int32, hi.shape, 1)
    line = lax.broadcasted_iota(jnp.int32, hi.shape, 0)
    for k in range(6):
        row = acc[k]
        row = jnp.sum(row[:, :lanes] + row[:, lanes:], axis=0, keepdims=True)
        hi = jnp.where(line == k, row, hi)
    grid = 192.0 * jnp.max(jnp.abs(hi), axis=1, keepdims=True)
    coarse = (hi + grid) - grid
    hi, lo = two_sum(
        jnp.sum(coarse, axis=1, keepdims=True), jnp.sum(hi - coarse, axis=1, keepdims=True))
    packed = jnp.where(lane == line, hi, 0.0) + jnp.where(lane == line + 8, lo, 0.0)
    tile[...] = jnp.sum(packed, axis=0, keepdims=True)

    def merge(total, lost):
        return total + jnp.where(lane[:1] >= 8, pltpu.roll(lost, 8, 1), 0.0)

    def row_to(source, rows, k, send, got, to):
        return pltpu.make_async_remote_copy(
            src_ref=source, dst_ref=rows.at[k], send_sem=send, recv_sem=got,
            device_id=to, device_id_type=MESH)

    def all_rows(rows, send, got):
        return pltpu.make_async_remote_copy(
            src_ref=rows, dst_ref=rows, send_sem=send, recv_sem=got,
            device_id=across(0), device_id_type=MESH)

    def summed(own, rows):
        total, lost = own, jnp.zeros(own.shape, jnp.float32)
        for k in range(rows.shape[0]):
            total, e = two_sum(total, rows[k])
            lost = lost + e
        return merge(total, lost)

    for k in range(len(wide)):
        row_to(tile, tiles, k, send_1, got_1, across(k)).start()
    all_rows(tiles, send_1, got_1).wait_recv()
    pair[...] = summed(tile[...], tiles)
    for k in range(len(up)):
        row_to(pair, pairs, k, send_2, got_2, beside(k)).start()
    all_rows(tiles, send_1, got_1).wait_send()

    @pl.when(is_outer)
    def _():
        for c in range(PIECES):
            send_b(c).wait_send()
            send_u(c).wait_send()

        @pl.when(late_half)
        def _():
            for c in from_late:
                send_p(c).wait_send()
                send_r(c).wait_send()

        @pl.when(early_half)
        def _():
            for c in from_early:
                send_w(c).wait_send()

    sigma, weight = quadrature(SH_DEV * n_shift, tile.shape)
    all_rows(pairs, send_2, got_2).wait_recv()
    total = summed(pair[...], pairs)
    total = jnp.broadcast_to(total, lane.shape)
    hi = jnp.sum(jnp.where(lane == line, total, 0.0), axis=1, keepdims=True)
    lo = jnp.sum(jnp.where(lane == line + 8, total, 0.0), axis=1, keepdims=True)
    hi, lo = jnp.broadcast_to(hi, lane.shape), jnp.broadcast_to(lo, lane.shape)
    hi, lo = quick(hi, lo)
    moments = [(hi[k : k + 1], lo[k : k + 1]) for k in range(6)]
    c0, c1, c2 = coefficients(moments, sigma, weight)

    for k in range(2):
        def body(c, k=k):
            value = c0 * flat(bb, k + 2, c) + c1 * flat(v1, k + 1, c) + c2 * flat(v2, k, c)
            out[k + high * (1 - 2 * k), rows_of(c)] = value

        each(body)
    all_rows(pairs, send_2, got_2).wait_send()


def on_device(state, reaction):
    n_space, n_shift = lax.axis_size("space"), lax.axis_size("shift")
    planes, rows, width = state.shape
    column = 2 * n_shift
    columns = n_space * n_shift // column
    piece = rows // PIECES
    f32 = jnp.float32
    padded = rows + 2 * PAD
    dma = pltpu.SemaphoreType.DMA
    cells = 2 * rows * width
    return pl.pallas_call(
        functools.partial(kernel, n_space, n_shift, column),
        out_shape=pltpu.VMEM((planes // n_shift, rows, width), f32),
        in_specs=[pl.BlockSpec(memory_space=pltpu.HBM)] * 2,
        out_specs=pl.BlockSpec(memory_space=pltpu.VMEM),
        scratch_shapes=[
            pltpu.VMEM((7, padded, width), f32),
            pltpu.VMEM((5, rows, width), f32),
            pltpu.VMEM((5, padded, width), f32),
            pltpu.VMEM((3, padded, width), f32),
            pltpu.VMEM((1, padded, width), f32),
            pltpu.VMEM((PIECES, piece, width), f32),
            pltpu.VMEM((PIECES, piece, width), f32),
            pltpu.VMEM((PIECES, piece, width), f32),
            pltpu.VMEM((PIECES, piece, width), f32),
            pltpu.VMEM((PIECES, piece, width), f32),
            pltpu.VMEM((PIECES, piece, width), f32),
            pltpu.VMEM((6, 8, width), f32),
            pltpu.VMEM((1, width // 2), f32),
            pltpu.VMEM((columns - 1, 1, width // 2), f32),
            pltpu.VMEM((1, width // 2), f32),
            pltpu.VMEM((column - 1, 1, width // 2), f32),
            dma((7,)),
            dma((5,)),
            dma((4 * PIECES,)),
            dma((PIECES,)),
            dma((PIECES,)),
            dma((PIECES,)),
            dma((PIECES,)),
            dma,
            dma,
            dma,
            dma,
        ],
        compiler_params=pltpu.CompilerParams(
            collective_id=0, has_side_effects=True, vmem_limit_bytes=58 * 2**20),
        cost_estimate=pl.CostEstimate(
            flops=100 * cells, bytes_accessed=40 * cells, transcendentals=0),
    )(state, reaction)


def solution(mesh):
    in_specs = (P("space", None, None), P("space", None, None))
    out_specs = P(("space", "shift"), None, None)
    return jax.shard_map(
        on_device, mesh=mesh, in_specs=in_specs, out_specs=out_specs, check_vma=False
    )
```
